512 devices in a mesh: seq: 32 (over z, core), head: 4 (over x), dp: 4 (over y).
Axes of the slice: x: 4, y: 4, z: 16, core: 2. Of those that a mesh axis runs over, the one named last changes fastest.
Arguments:
- passthrough: bfloat16 [4, 8192, 1024], P('dp', 'seq', 'head'), may hold values from -6 to 6
- mixed_out: bfloat16 [4, 8192, 1024], P('dp', 'seq', 'head'), may hold values from -6 to 6
- grad_mixed: bfloat16 [4, 8192, 1024], P('dp', 'seq', 'head'), may hold values from -6 to 6
- grad_pass: bfloat16 [4, 8192, 1024], P('dp', 'seq', 'head'), may hold values from -6 to 6
- query_weight: bfloat16 [1024, 1024], P(None, 'head'), may hold values from -0.1875 to 0.1875
- key_weight: bfloat16 [1024, 1024], P(None, 'head'), may hold values from -0.1875 to 0.1875
- value_weight: bfloat16 [1024, 1024], P(None, 'head'), may hold values from -0.1875 to 0.1875
- random_features: bfloat16 [8, 128, 256], P('head'), may hold values from -5 to 5
- document_ids: int32 [4, 8192], P('dp', 'seq'), may hold values from 0 to 27, never falling along the last dimension, each value on 1 to 2048 neighbouring positions
Outputs:
- first_in: bfloat16 [4, 8192, 1024], P('dp', 'seq', 'head')
- grad_second: bfloat16 [4, 8192, 1024], P('dp', 'seq', 'head')
- grad_query_weight: float32 [1024, 1024], P(('seq', 'dp'), 'head')
- grad_key_weight: float32 [1024, 1024], P(('seq', 'dp'), 'head')
- grad_value_weight: float32 [1024, 1024], P(('seq', 'dp'), 'head')
The draws below stay inside these ranges and needn't reach their ends.
Inputs may be any that keep to these rules, and one draw needn't show every extreme that they name: `document_ids`: along each context the number never falls; each of the 28 documents holds 1 to 2048 positions, and one holds exactly 2048.
All inputs are finite; a program needn't handle non-finite values.
Results may differ from the reference program's by a relative error of at most 0.018.
The reference program's roundings to bfloat16 on the way count: a program that leaves them out, or rounds other values in their place, can miss the bound.
Values may be sent and summed in bfloat16 or wider, within the bound.
A program may use at most 64 MiB of HBM per device.

```python
import math
import jax
import jax.numpy as jnp
import numpy as np
from jax import lax

D = 1024
HEADS = 8
HD = 128
FEAT = 256
TOK_DEV = 256
SEQ = 8192
CTXS = 4
DOCS = 28
MOST = 2048
N_SEQ = 32
N_HEAD = 4


def spiked(array, rng, source, target, shards_of, factor):
    def block_of(position):
        return (jnp.arange(array.shape[position]) // (array.shape[position] // shards_of)).reshape((-1,) + (1,) * (array.ndim - 1 - position))

    near = jax.random.permutation(rng, shards_of)[block_of(target)]
    far = (block_of(target) + shards_of // 2) % shards_of
    return jnp.where((block_of(source) == near) | (block_of(source) == far), factor * array, array)


def shard_levels(rng, extent, cuts, low, high):
    def one(dim, parts):
        draws = jax.random.uniform(jax.random.fold_in(jax.random.fold_in(rng, 6), dim), (parts,), jnp.float32, low / len(cuts), high / len(cuts))
        return jnp.repeat(jnp.exp(draws), extent[dim] // parts).reshape((-1,) + (1,) * (len(extent) - dim - 1))

    gain = one(*cuts[0])
    for cut in cuts[1:]:
        gain = gain * one(*cut)
    return gain


def split_up(number_of, total, most, skew):
    weights = [(1 << 20) // math.isqrt(rank ** skew) + 1 for rank in range(2, number_of + 1)]
    spare, counts = total - most - (number_of - 1), [1] * (number_of - 1)
    while spare > 0:
        movable = [i for i in range(number_of - 1) if counts[i] < most]
        whole, left = sum([weights[i] for i in movable]), spare
        for i in movable:
            more = min(most - counts[i], max(1, left * weights[i] // whole), spare)
            counts[i] = counts[i] + more
            spare = spare - more
    return np.array([most] + counts)


def ragged(own_key, amount, total, bound, slope):
    if amount == 2:
        one = jax.random.randint(own_key, (), max(1, total - bound), min(bound, total - 1) + 1)
        return jnp.stack([one, total - one])
    lengths = jnp.asarray(split_up(amount, total, bound, slope), jnp.int32)
    pairs = (amount - 1) // 2
    giver, taker = lengths[1:1 + 2 * pairs:2], lengths[2:2 + 2 * pairs:2]
    slack = jnp.minimum(giver - 1, bound - taker)
    moved = jax.random.randint(jax.random.fold_in(own_key, 1), (pairs,), 0, 1 << 20) % (slack + 1)
    lengths = lengths.at[1:1 + 2 * pairs:2].set(giver - moved).at[2:2 + 2 * pairs:2].set(taker + moved)
    return lengths[jax.random.permutation(jax.random.fold_in(own_key, 2), amount)]


def gaussian(key, dims, spread, bound, pieces=(), kind=jnp.bfloat16):
    array = jax.random.normal(key, dims, jnp.float32) * spread
    if len(pieces) > 0:
        array = shard_levels(key, dims, pieces, -0.22, 0.18) * array
    return jnp.clip(array, min=-bound, max=bound).astype(kind)


def heavy_noise(key, dims, scale, bound, pieces, heavy, held_as=jnp.bfloat16):
    array = scale * jax.random.normal(key, dims, jnp.float32)
    if pieces:
        array = array * shard_levels(key, dims, pieces, -0.22, 0.18)
    return jnp.clip(spiked(array, jax.random.fold_in(key, 3), *heavy), -bound, bound).astype(held_as)


def setup_inputs(seed: int = 0) -> dict:
    key_of = jax.random.split(jax.random.key(seed), 10)
    return {
        "passthrough": heavy_noise(key_of[0], (CTXS, SEQ, D), 1.0, 6.0, ((0, 4), (1, 32), (2, 4)), (1, 2, 32, 2.75)),
        "mixed_out": gaussian(key_of[1], (CTXS, SEQ, D), 1.0, 6.0, ((0, 4), (1, 32), (2, 4))),
        "grad_mixed": gaussian(key_of[2], (CTXS, SEQ, D), 1.0, 6.0, ((0, 4), (1, 32), (2, 4))),
        "grad_pass": gaussian(key_of[3], (CTXS, SEQ, D), 1.0, 6.0, ((0, 4), (1, 32), (2, 4))),
        "query_weight": gaussian(key_of[4], (D, D), D ** -0.5, 0.1875, ((1, 4),)),
        "key_weight": gaussian(key_of[5], (D, D), D ** -0.5, 0.1875, ((1, 4),)),
        "value_weight": gaussian(key_of[6], (D, D), D ** -0.5, 0.1875, ((1, 4),)),
        "random_features": gaussian(key_of[7], (HEADS, HD, FEAT), 1.0, 5.0, ((0, 4),)),
        "document_ids": jax.vmap(lambda own: jnp.searchsorted(jnp.cumsum(ragged(own, DOCS, SEQ, MOST, 2)), jnp.arange(SEQ), side="right"))(jax.random.split(key_of[8], CTXS)).reshape((CTXS, SEQ)).astype(jnp.int32),
    }


EPSILON = 1e-06
HIGHEST = lax.Precision.HIGHEST

def to_blocks(matrix):
    return matrix.reshape(N_SEQ, TOK_DEV, HEADS, HD).transpose(0, 2, 1, 3)

def from_blocks(tensor):
    return tensor.transpose(0, 2, 1, 3).reshape(N_SEQ * TOK_DEV, HEADS * HD)

def feature_map(projected, random_features):
    mixing = jnp.einsum('bhtd,hdm->bhtm', projected.astype(jnp.float32), random_features.astype(jnp.float32))
    widened = projected.astype(jnp.float32)
    squares = lax.optimization_barrier(jnp.sum(widened * widened, axis=-1, keepdims=True))
    exponent = mixing / HD ** 0.25 - squares / (2.0 * HD ** 0.5)
    return (jnp.exp(exponent) / FEAT ** 0.5).astype(jnp.bfloat16)

def feature_grad(dfeature, feature, projected, random_features):
    dexponent = dfeature * feature.astype(jnp.float32)
    rounded = dexponent.astype(jnp.bfloat16)
    back_proj = jnp.einsum('bhtm,hdm->bhtd', rounded.astype(jnp.float32), random_features.astype(jnp.float32))
    totals = lax.optimization_barrier(jnp.sum(dexponent, axis=-1, keepdims=True))
    result = back_proj / HD ** 0.25 - projected.astype(jnp.float32) * totals / HD ** 0.5
    return result.astype(jnp.bfloat16)

def carry_step(carry, element):
    state_in, state_id = carry
    block_state, block_id = element
    merged = block_state + jnp.where(state_id == block_id, state_in, jnp.zeros_like(state_in))
    return ((merged, block_id), carry)

def one_context(inputs, query_weight, key_weight, value_weight, random_features):
    passthrough, mixed_out, grad_mixed, grad_pass, doc_row = inputs
    widened = passthrough.astype(jnp.float32)
    inv_rms = lax.rsqrt(lax.optimization_barrier(jnp.mean(widened * widened, axis=-1, keepdims=True)) + EPSILON)
    norm_exact = widened * inv_rms
    normed = norm_exact.astype(jnp.bfloat16)
    query_all = jnp.dot(normed, query_weight, preferred_element_type=jnp.float32).astype(jnp.bfloat16)
    key_all = jnp.dot(normed, key_weight, preferred_element_type=jnp.float32).astype(jnp.bfloat16)
    value_all = jnp.dot(normed, value_weight, preferred_element_type=jnp.float32).astype(jnp.bfloat16)
    query_heads = to_blocks(query_all)
    key_heads = to_blocks(key_all)
    value_heads = to_blocks(value_all)
    feat_query = feature_map(query_heads, random_features)
    feat_key = feature_map(key_heads, random_features)
    fq_wide = feat_query.astype(jnp.float32)
    fk_wide = feat_key.astype(jnp.float32)
    value_wide = value_heads.astype(jnp.float32)
    block_ids = doc_row.reshape(N_SEQ, TOK_DEV).astype(jnp.int32)
    rows_idx = lax.broadcasted_iota(jnp.int32, (TOK_DEV, TOK_DEV), 0)
    cols_idx = lax.broadcasted_iota(jnp.int32, (TOK_DEV, TOK_DEV), 1)
    allowed = ((block_ids[:, :, None] == block_ids[:, None, :]) & (rows_idx >= cols_idx)[None])[:, None]
    scores = jnp.einsum('bhtm,bhsm->bhts', fq_wide, fk_wide)
    pair_weight = jnp.where(allowed, scores, 0.0).astype(jnp.bfloat16)
    pair_wide = pair_weight.astype(jnp.float32)
    attn_local = jnp.einsum('bhts,bhsd->bhtd', pair_wide, value_wide)
    last_ids = block_ids[:, -1]
    tail_mask = (block_ids == last_ids[:, None])[:, None, :, None]
    tail_state = jnp.einsum('bhtm,bhtd->bhmd', jnp.where(tail_mask, fk_wide, 0.0), value_wide)
    empty_state = jnp.zeros((HEADS, FEAT, HD), jnp.float32)
    _, (state_in, state_id) = lax.scan(carry_step, (empty_state, jnp.int32(-1)), (tail_state, last_ids))
    head_on = (block_ids == state_id[:, None])[:, None, :, None]
    carried = jnp.einsum('bhtm,bhmd->bhtd', fq_wide, state_in, precision=HIGHEST)
    attention = attn_local + jnp.where(head_on, carried, 0.0)
    inv_attn = lax.rsqrt(lax.optimization_barrier(jnp.mean(attention * attention, axis=-1, keepdims=True)) + EPSILON)
    act = attention * inv_attn
    first_in = (mixed_out.astype(jnp.float32) - from_blocks(act)).astype(jnp.bfloat16)
    grad_act = to_blocks(grad_mixed).astype(jnp.float32)
    grad_attn = (inv_attn * (grad_act - act * lax.optimization_barrier(jnp.mean(grad_act * act, axis=-1, keepdims=True)))).astype(jnp.bfloat16)
    grad_wide = grad_attn.astype(jnp.float32)
    dscores = jnp.einsum('bhtd,bhsd->bhts', grad_wide, value_wide)
    dpair = jnp.where(allowed, dscores, 0.0).astype(jnp.bfloat16).astype(jnp.float32)
    first_ids = block_ids[:, 0]
    head_mask = (block_ids == first_ids[:, None])[:, None, :, None]
    head_state = jnp.einsum('bhtm,bhtd->bhmd', jnp.where(head_mask, fq_wide, 0.0), grad_wide)
    _, (state_later, later_id) = lax.scan(carry_step, (empty_state, jnp.int32(-1)), (head_state, first_ids), reverse=True)
    tail_on = (block_ids == later_id[:, None])[:, None, :, None]
    dfeat_query = jnp.einsum('bhts,bhsm->bhtm', dpair, fk_wide)
    dfeat_query = dfeat_query + jnp.where(head_on, jnp.einsum('bhtd,bhmd->bhtm', grad_wide, state_in, precision=HIGHEST), 0.0)
    dfeat_key = jnp.einsum('bhts,bhtm->bhsm', dpair, fq_wide)
    dfeat_key = dfeat_key + jnp.where(tail_on, jnp.einsum('bhsd,bhmd->bhsm', value_wide, state_later, precision=HIGHEST), 0.0)
    dvalue = jnp.einsum('bhts,bhtd->bhsd', pair_wide, grad_wide)
    dvalue = (dvalue + jnp.where(tail_on, jnp.einsum('bhsm,bhmd->bhsd', fk_wide, state_later, precision=HIGHEST), 0.0)).astype(jnp.bfloat16)
    dquery = feature_grad(dfeat_query, feat_query, query_heads, random_features)
    dkey = feature_grad(dfeat_key, feat_key, key_heads, random_features)
    dquery_flat = from_blocks(dquery)
    dkey_flat = from_blocks(dkey)
    dvalue_flat = from_blocks(dvalue)
    group_width = D // N_HEAD
    grad_normed = jnp.zeros((N_SEQ * TOK_DEV, D), jnp.float32)
    for group in range(N_HEAD):
        low = group * group_width
        high = low + group_width
        term = jnp.dot(dquery_flat[:, low:high], query_weight[:, low:high].T, preferred_element_type=jnp.float32)
        term = term + jnp.dot(dkey_flat[:, low:high], key_weight[:, low:high].T, preferred_element_type=jnp.float32)
        term = term + jnp.dot(dvalue_flat[:, low:high], value_weight[:, low:high].T, preferred_element_type=jnp.float32)
        grad_normed = grad_normed + term.astype(jnp.bfloat16).astype(jnp.float32)
    dot_mean = lax.optimization_barrier(jnp.mean(grad_normed * norm_exact, axis=-1, keepdims=True))
    grad_second = (grad_pass.astype(jnp.float32) + inv_rms * (grad_normed - norm_exact * dot_mean)).astype(jnp.bfloat16)
    stacked = jnp.concatenate([dquery_flat, dkey_flat, dvalue_flat], axis=1)
    weight_term = jnp.dot(normed.T, stacked, preferred_element_type=jnp.float32)
    return (first_in, grad_second, weight_term)

def reference(passthrough, mixed_out, grad_mixed, grad_pass, query_weight, key_weight, value_weight, random_features, document_ids):

    def per_context(inputs):
        return one_context(inputs, query_weight, key_weight, value_weight, random_features)
    first_in, grad_second, weight_terms = lax.map(per_context, (passthrough, mixed_out, grad_mixed, grad_pass, document_ids))
    summed = lax.optimization_barrier(jnp.sum(weight_terms, axis=0)) / (CTXS * SEQ) ** 0.5
    return (first_in, grad_second, summed[:, :D], summed[:, D:2 * D], summed[:, 2 * D:])
```

```python
import functools

import jax
import jax.numpy as jnp
from jax import lax
from jax.experimental import pallas as pl
from jax.experimental.pallas import tpu as pltpu
from jax.sharding import PartitionSpec as P

MESH = pl.DeviceIdType.MESH
BF = jnp.bfloat16
F32 = jnp.float32
EPSILON = 1e-06
TOK = 256
D = 1024
WID = 256
HD = 128
FEAT = 256
IDR = 16
MSG = FEAT + IDR
NX = 4


def nn(a, b):
    return jnp.dot(a, b, preferred_element_type=F32)


def nt(a, b):
    return lax.dot_general(a, b, (((1,), (1,)), ((), ())), preferred_element_type=F32)


def tn(a, b):
    return lax.dot_general(a, b, (((0,), (0,)), ((), ())), preferred_element_type=F32)


def kernel(
    nz,
    ny,
    grad_scale,
    pt_h,
    mo_h,
    gm_h,
    gp_h,
    wq_h,
    wk_h,
    wv_h,
    rf_h,
    ids_h,
    fi_o,
    gs_o,
    oq_o,
    ok_o,
    ov_o,
    xs,
    mo,
    gm,
    gp,
    w3,
    rf,
    ids,
    nrm,
    ntp,
    nts,
    qkv,
    fq,
    fk,
    pair,
    ga,
    dfk,
    dvl,
    dqkv,
    dqs,
    fmsg,
    fsib,
    fchip,
    fr,
    fs2,
    fst,
    foth,
    bmsg,
    bsib,
    bchip,
    br,
    bs2,
    bst,
    both,
    xso,
    xsm,
    xro,
    xrm,
    dots,
    dotr,
    qso,
    qsm,
    qro,
    qrm,
    kso,
    ksm,
    kro,
    krm,
    zqs,
    zqr,
    zks,
    zkr,
    lsem,
    ssem,
    rsem,
):
    seq = lax.axis_index("seq")
    x = lax.axis_index("head")
    y = lax.axis_index("dp")
    z = seq // 2
    c = seq % 2
    oc = 1 - c
    rw = D // (2 * nz * ny)
    rows_y = nz * rw
    right = lax.rem(x + 1, NX)
    left = lax.rem(x + NX - 1, NX)
    opp = lax.rem(x + 2, NX)

    def at_x(other):
        return (seq, other, y)

    def at_y(other):
        return (seq, x, other)

    def at_z(step):
        return (lax.rem(z + step + nz, nz) * 2 + c, x, y)

    sibling = (z * 2 + oc, x, y)

    barrier = pltpu.get_barrier_semaphore()
    peers = [sibling]
    peers += [at_x(lax.rem(x + d, NX)) for d in range(1, NX)]
    peers += [at_y(lax.rem(y + d, ny)) for d in range(1, ny)]
    peers += [at_z(d) for d in range(1, nz)]
    for peer in peers:
        pl.semaphore_signal(barrier, inc=1, device_id=peer, device_id_type=MESH)

    local = [
        pltpu.make_async_copy(src, dst, lsem.at[i])
        for i, (src, dst) in enumerate(
            [
                (pt_h.at[0], xs.at[0]),
                (ids_h, ids),
                (wk_h, w3.at[1]),
                (wv_h, w3.at[2]),
                (rf_h, rf),
                (wq_h, w3.at[0]),
                (gm_h.at[0], gm),
                (mo_h.at[0], mo),
                (gp_h.at[0], gp),
            ]
        )
    ]
    for copy in local:
        copy.start()

    counter = [0]
    pending = []

    def send(src, dst, device):
        i = counter[0]
        counter[0] += 1
        copy = pltpu.make_async_remote_copy(
            src_ref=src,
            dst_ref=dst,
            send_sem=ssem.at[i],
            recv_sem=rsem.at[i],
            device_id=device,
            device_id_type=MESH,
        )
        copy.start()
        pending.append(copy)
        return copy

    local[0].wait()
    pl.semaphore_wait(barrier, len(peers))

    top, bot = pl.ds(0, TOK // 2), pl.ds(TOK // 2, TOK // 2)
    l_top = send(xs.at[0, top], xs.at[1, top], at_x(right))
    r_bot = send(xs.at[0, bot], xs.at[3, bot], at_x(left))
    l_bot = send(xs.at[0, bot], xs.at[1, bot], at_x(right))
    r_top = send(xs.at[0, top], xs.at[3, top], at_x(left))

    local[1].wait()
    ids_row = jnp.broadcast_to(ids[...].astype(F32), (TOK, TOK))
    ids_col = ids_row.T
    tri = lax.broadcasted_iota(jnp.int32, (TOK, TOK), 0) >= lax.broadcasted_iota(
        jnp.int32, (TOK, TOK), 1
    )
    allowed = (ids_row == ids_col) & tri
    col_ids = ids_col[:, :HD]
    last_id = ids_row[:, TOK - 1 : TOK]
    first_id = ids_row[:, 0:1]
    is_last = col_ids == last_id
    is_first = col_ids == first_id
    last_rows = jnp.broadcast_to(last_id[:IDR], (IDR, HD)).astype(BF)
    first_rows = jnp.broadcast_to(first_id[:IDR], (IDR, HD)).astype(BF)

    l_top.wait_recv()
    o_top = send(xs.at[1, top], xs.at[2, top], at_x(right))
    r_bot.wait_recv()
    o_bot = send(xs.at[3, bot], xs.at[2, bot], at_x(left))

    def square_sum(slot):
        wide = xs[slot].astype(F32)
        return jnp.sum(wide * wide, axis=1, keepdims=True)

    squares = square_sum(0)
    l_bot.wait_recv()
    squares = squares + square_sum(1)
    r_top.wait_recv()
    squares = squares + square_sum(3)
    o_top.wait_recv()
    o_bot.wait_recv()
    squares = squares + square_sum(2)
    inv_rms = lax.rsqrt(squares * (1.0 / D) + EPSILON)
    for slot in range(NX):
        nrm[slot] = (xs[slot].astype(F32) * inv_rms).astype(BF)

    def source(slot):
        return lax.rem(x + NX - slot, NX)

    def project(which):
        total = None
        for slot in range(NX):
            rows = pl.ds(pl.multiple_of(source(slot) * WID, WID), WID)
            term = nn(nrm[slot], w3[which, rows, :])
            total = term if total is None else total + term
        return total.astype(BF)

    def features(head, projected):
        wide = projected.astype(F32)
        norm = jnp.sum(wide * wide, axis=1, keepdims=True)
        exponent = nn(projected, rf[head]) * (1.0 / HD**0.25) - norm * (1.0 / (2.0 * HD**0.5))
        return (jnp.exp(exponent) * (1.0 / FEAT**0.5)).astype(BF)

    local[2].wait()
    local[3].wait()
    local[4].wait()
    key = project(1)
    value = project(2)
    for head in range(2):
        cols = slice(head * HD, (head + 1) * HD)
        qkv[1, head] = key[:, cols]
        qkv[2, head] = value[:, cols]
        fk[head] = features(head, key[:, cols])
        masked = jnp.where(is_last, value[:, cols].astype(F32), 0.0).astype(BF)
        fmsg[head, 0:FEAT] = tn(fk[head], masked).astype(BF)
        fmsg[head, FEAT:MSG] = last_rows

    def merge(near, far):
        near_id, far_id = near[FEAT : FEAT + 1], far[FEAT : FEAT + 1]
        joined = near[:FEAT] + jnp.where(near_id == far_id, far[:FEAT], 0.0)
        return jnp.concatenate([joined, near[FEAT:]], axis=0)

    class Scan:
        def __init__(self, forward, msg, sib, chip, got, two, state, other):
            self.sign = 1 if forward else -1
            self.first = c == (0 if forward else 1)
            self.msg, self.sib, self.chip, self.got = msg, sib, chip, got
            self.two, self.state, self.other = two, state, other

        def begin(self):
            self.c0 = send(self.msg.at[oc], self.sib, sibling)

        def chips(self):
            self.c0.wait_recv()
            own, sib = self.msg[c].astype(F32), self.sib[...].astype(F32)
            upper = jnp.where(self.first, own, sib)
            lower = jnp.where(self.first, sib, own)
            self.chip[...] = merge(lower, upper).astype(BF)
            self.c1 = send(self.chip, self.got.at[0], at_z(self.sign))
            self.c2 = send(self.chip, self.got.at[1], at_z(2 * self.sign))

        def pairs(self):
            self.c1.wait_recv()
            self.c2.wait_recv()
            near, far = self.got[0].astype(F32), self.got[1].astype(F32)
            self.two[...] = merge(near, far).astype(BF)
            self.c3 = send(self.two, self.got.at[2], at_z(2 * self.sign))

        def spread(self):
            self.c3.wait_recv()
            own, sib = self.msg[c].astype(F32), self.sib[...].astype(F32)
            upper = jnp.where(self.first, own, sib)
            before = merge(self.two[...].astype(F32), self.got[2].astype(F32))
            after = merge(upper, before)
            self.state[c] = jnp.where(self.first, before, after).astype(BF)
            self.other[...] = jnp.where(self.first, after, before).astype(BF)
            self.c4 = send(self.other, self.state.at[c], sibling)

        def finish(self):
            self.c4.wait_recv()

    forward = Scan(True, fmsg, fsib, fchip, fr, fs2, fst, foth)
    forward.begin()

    local[5].wait()
    query = project(0)
    for head in range(2):
        cols = slice(head * HD, (head + 1) * HD)
        qkv[0, head] = query[:, cols]

    forward.chips()

    for head in range(2):
        fq[head] = features(head, qkv[0, head])
        scores = nt(fq[head], fk[head])
        pair[head] = jnp.where(allowed, scores, 0.0).astype(BF)

    forward.pairs()

    per_slot = nz // NX
    for slot in range(NX):
        turned = (xs[slot].astype(F32) * inv_rms).T.reshape(per_slot, 2, ny, rw, TOK)
        place = pl.ds(pl.multiple_of(source(slot) * (per_slot * rw), per_slot * rw), per_slot * rw)
        for core in range(2):
            for part in range(ny):
                block = turned[:, core, part].reshape(per_slot * rw, TOK)
                ntp[core, part, place, :] = block.astype(BF)
    c_nt = send(ntp.at[oc], nts, sibling)
    attn_local = [nn(pair[head], qkv[2, head]) for head in range(2)]

    forward.spread()
    local[6].wait()
    local[7].wait()
    forward.finish()

    for head in range(2):
        cols = slice(head * HD, (head + 1) * HD)
        on = col_ids == fst[head, FEAT : FEAT + 1, :].astype(F32)
        carried = nn(fq[head], fst[head, 0:FEAT, :])
        attention = attn_local[head] + jnp.where(on, carried, 0.0)
        inv_attn = lax.rsqrt(jnp.mean(attention * attention, axis=1, keepdims=True) + EPSILON)
        act = attention * inv_attn
        grad_act = gm[:, cols].astype(F32)
        inner = jnp.mean(grad_act * act, axis=1, keepdims=True)
        grad_wide = (inv_attn * (grad_act - act * inner)).astype(BF)
        ga[head] = grad_wide
        masked = jnp.where(is_first, grad_wide.astype(F32), 0.0).astype(BF)
        bmsg[head, 0:FEAT] = tn(fq[head], masked).astype(BF)
        bmsg[head, FEAT:MSG] = first_rows
        fi_o[0, :, cols] = (mo[:, cols].astype(F32) - act).astype(BF)

    backward = Scan(False, bmsg, bsib, bchip, br, bs2, bst, both)
    backward.begin()

    def feature_grad(dfeature, feature, projected, head):
        dexponent = dfeature * feature.astype(F32)
        back = nt(dexponent.astype(BF), rf[head])
        totals = jnp.sum(dexponent, axis=1, keepdims=True)
        result = back * (1.0 / HD**0.25) - projected.astype(F32) * (totals * (1.0 / HD**0.5))
        return result.astype(BF)

    dpairs = []
    for head in range(2):
        dscores = nt(ga[head], qkv[2, head])
        dpairs.append(jnp.where(allowed, dscores, 0.0).astype(BF))

    backward.chips()

    for head in range(2):
        cols = slice(head * HD, (head + 1) * HD)
        on = col_ids == fst[head, FEAT : FEAT + 1, :].astype(F32)
        masked = jnp.where(on, ga[head].astype(F32), 0.0).astype(BF)
        dfq = nn(dpairs[head], fk[head]) + nt(masked, fst[head, 0:FEAT, :])
        dqkv[0, :, cols] = feature_grad(dfq, fq[head], qkv[0, head], head)
    c_dq = send(dqkv.at[0], dqs.at[0], sibling)

    backward.pairs()

    for head in range(2):
        dfk[head] = tn(dpairs[head], fq[head])
        dvl[head] = tn(pair[head], ga[head])

    class Ring:
        def __init__(self, so, sm, ro, rm, to_right, to_left):
            self.so, self.sm, self.ro, self.rm = so, sm, ro, rm
            self.to_right, self.to_left = to_right, to_left
            self.half = so.shape[1]

        def opposite(self, block):
            self.so[0] = block[: self.half].astype(BF)
            self.so[1] = block[self.half :].astype(BF)
            self.o0 = send(self.so.at[0], self.ro.at[0], self.to_right)
            self.o1 = send(self.so.at[1], self.ro.at[1], self.to_left)

        def sides(self, to_right, to_left):
            self.sm[0, 1] = to_right[self.half :].astype(BF)
            self.m01 = send(self.sm.at[0, 1], self.rm.at[0, 1], self.to_right)
            self.sm[1, 0] = to_left[: self.half].astype(BF)
            self.m10 = send(self.sm.at[1, 0], self.rm.at[1, 0], self.to_left)
            self.r_top = to_right[: self.half]
            self.l_bot = to_left[self.half :]

        def relay(self):
            self.o0.wait_recv()
            self.sm[0, 0] = (self.r_top + self.ro[0].astype(F32)).astype(BF)
            self.m00 = send(self.sm.at[0, 0], self.rm.at[0, 0], self.to_right)
            self.o1.wait_recv()
            self.sm[1, 1] = (self.l_bot + self.ro[1].astype(F32)).astype(BF)
            self.m11 = send(self.sm.at[1, 1], self.rm.at[1, 1], self.to_left)

        def total(self, own):
            for copy in (self.m01, self.m10, self.m00, self.m11):
                copy.wait_recv()
            halves = [
                own[i * self.half : (i + 1) * self.half]
                + self.rm[0, i].astype(F32)
                + self.rm[1, i].astype(F32)
                for i in range(2)
            ]
            return jnp.concatenate(halves, axis=0)

    up, down = lax.rem(y + 1, ny), lax.rem(y + ny - 1, ny)

    def weight_rows(which, part):
        left_rows, right_rows = ntp[c, part], nts[part]
        term = nn(left_rows, dqkv[which]) + nn(right_rows, dqs[which])
        return term * grad_scale

    def y_block(whiches, part):
        return jnp.concatenate([weight_rows(which, part) for which in whiches], axis=1)

    def start_weights(ring, whiches):
        ring.opposite(y_block(whiches, lax.rem(y + 2, ny)))
        ring.sides(y_block(whiches, up), y_block(whiches, down))

    c_nt.wait_recv()
    c_dq.wait_recv()
    ring_q = Ring(qso, qsm, qro, qrm, at_y(up), at_y(down))
    if ny > 1:
        start_weights(ring_q, [0])
    own_q = y_block([0], y)

    backward.spread()
    if ny > 1:
        ring_q.relay()
    backward.finish()

    for head in range(2):
        cols = slice(head * HD, (head + 1) * HD)
        on = col_ids == bst[head, FEAT : FEAT + 1, :].astype(F32)
        later = bst[head, 0:FEAT, :]
        masked = jnp.where(on, qkv[2, head].astype(F32), 0.0).astype(BF)
        dfeat = dfk[head] + nt(masked, later)
        dqkv[2, :, cols] = (dvl[head] + jnp.where(on, nn(fk[head], later), 0.0)).astype(BF)
        dqkv[1, :, cols] = feature_grad(dfeat, fk[head], qkv[1, head], head)
    c_dkv = send(dqkv.at[pl.ds(1, 2)], dqs.at[pl.ds(1, 2)], sibling)

    def normed_term(owner, slot):
        rows = pl.ds(pl.multiple_of(owner * WID, WID), WID)
        term = nt(dqkv[0], w3[0, rows, :])
        term = term + nt(dqkv[1], w3[1, rows, :])
        term = term + nt(dqkv[2], w3[2, rows, :])
        return term, jnp.sum(term * xs[slot].astype(F32), axis=1, keepdims=True)

    ring_x = Ring(xso, xsm, xro, xrm, at_x(right), at_x(left))
    term, dot = normed_term(opp, 2)
    ring_x.opposite(term)
    term_r, dot_r = normed_term(right, 3)
    term_l, dot_l = normed_term(left, 1)
    ring_x.sides(term_r, term_l)

    c_dkv.wait_recv()
    ring_k = Ring(kso, ksm, kro, krm, at_y(up), at_y(down))
    if ny > 1:
        start_weights(ring_k, [1, 2])
    ring_x.relay()
    own_k = y_block([1, 2], y)

    term_own, dot_own = normed_term(x, 0)
    dot = (dot + dot_r + dot_l + dot_own) * inv_rms
    dots[...] = jnp.broadcast_to(dot, (TOK, HD)).T[:8]
    c_dot = [
        send(dots, dotr.at[d - 1], at_x(lax.rem(x + d, NX))) for d in range(1, NX)
    ]

    def z_send(out, got):
        copies = []
        for d in range(1, nz):
            to = lax.rem(z + d, nz)
            copies.append(send(out.at[to], got.at[d], at_z(d)))
        return copies

    def z_total(copies, out, got):
        total = out[z].astype(F32)
        for d in range(1, nz):
            copies[d - 1].wait_recv()
            total = total + got[d].astype(F32)
        return total

    total_q = ring_q.total(own_q) if ny > 1 else own_q
    total_q = total_q.reshape(nz, rw, WID)
    zqs[...] = jnp.concatenate([total_q[:, :, :HD], total_q[:, :, HD:]], axis=1).astype(BF)
    z_q = z_send(zqs, zqr)

    if ny > 1:
        ring_k.relay()

    for copy in c_dot:
        copy.wait_recv()
    dot_rows = dots[...] + dotr[0] + dotr[1] + dotr[2]
    dot_all = jnp.broadcast_to(dot_rows[0:1], (HD, TOK)).T
    local[8].wait()
    grad_normed = ring_x.total(term_own)
    norm_own = xs[0].astype(F32) * inv_rms
    mean = dot_all[:, 0:1] * (1.0 / D)
    gs_o[0] = (gp[...].astype(F32) + inv_rms * (grad_normed - norm_own * mean)).astype(BF)

    total_k = ring_k.total(own_k) if ny > 1 else own_k
    part_k = total_k[:, :WID].reshape(nz, rw, WID)
    part_v = total_k[:, WID:].reshape(nz, rw, WID)
    zks[...] = jnp.concatenate([part_k, part_v], axis=1).astype(BF)
    z_k = z_send(zks, zkr)

    sum_q = z_total(z_q, zqs, zqr)
    oq_o[...] = jnp.concatenate([sum_q[:rw], sum_q[rw:]], axis=1)
    sum_k = z_total(z_k, zks, zkr)
    ok_o[...] = sum_k[:rw]
    ov_o[...] = sum_k[rw:]

    for copy in pending:
        copy.wait_send()


def solution(mesh):
    nz = mesh.shape["seq"] // 2
    ny = mesh.shape["dp"]
    rw = D // (2 * nz * ny)
    rows_y = nz * rw

    def ring(rows, columns):
        half = rows // 2
        return [
            pltpu.VMEM((2, half, columns), BF),
            pltpu.VMEM((2, 2, half, columns), BF),
            pltpu.VMEM((2, half, columns), BF),
            pltpu.VMEM((2, 2, half, columns), BF),
        ]

    scan = [
        pltpu.VMEM((2, MSG, HD), BF),
        pltpu.VMEM((MSG, HD), BF),
        pltpu.VMEM((MSG, HD), BF),
        pltpu.VMEM((3, MSG, HD), BF),
        pltpu.VMEM((MSG, HD), BF),
        pltpu.VMEM((2, MSG, HD), BF),
        pltpu.VMEM((MSG, HD), BF),
    ]

    def shards(pt, mo, gm, gp, wq, wk, wv, rf, ids):
        total_rows = TOK * 2 * nz * ny
        copies = 100
        return pl.pallas_call(
            functools.partial(kernel, nz, ny, 1.0 / total_rows**0.5),
            out_shape=(
                jax.ShapeDtypeStruct((1, TOK, WID), BF),
                jax.ShapeDtypeStruct((1, TOK, WID), BF),
                jax.ShapeDtypeStruct((rw, WID), F32),
                jax.ShapeDtypeStruct((rw, WID), F32),
                jax.ShapeDtypeStruct((rw, WID), F32),
            ),
            in_specs=[pl.BlockSpec(memory_space=pl.ANY)] * 9,
            out_specs=[pl.BlockSpec(memory_space=pltpu.VMEM)] * 5,
            scratch_shapes=[
                pltpu.VMEM((NX, TOK, WID), BF),
                pltpu.VMEM((TOK, WID), BF),
                pltpu.VMEM((TOK, WID), BF),
                pltpu.VMEM((TOK, WID), BF),
                pltpu.VMEM((3, D, WID), BF),
                pltpu.VMEM((2, HD, FEAT), BF),
                pltpu.VMEM((1, TOK), jnp.int32),
                pltpu.VMEM((NX, TOK, WID), BF),
                pltpu.VMEM((2, ny, rows_y, TOK), BF),
                pltpu.VMEM((ny, rows_y, TOK), BF),
                pltpu.VMEM((3, 2, TOK, HD), BF),
                pltpu.VMEM((2, TOK, FEAT), BF),
                pltpu.VMEM((2, TOK, FEAT), BF),
                pltpu.VMEM((2, TOK, TOK), BF),
                pltpu.VMEM((2, TOK, HD), BF),
                pltpu.VMEM((2, TOK, FEAT), F32),
                pltpu.VMEM((2, TOK, HD), F32),
                pltpu.VMEM((3, TOK, WID), BF),
                pltpu.VMEM((3, TOK, WID), BF),
                *scan,
                *scan,
                *ring(TOK, WID),
                pltpu.VMEM((8, TOK), F32),
                pltpu.VMEM((NX - 1, 8, TOK), F32),
                *ring(rows_y, WID),
                *ring(rows_y, 2 * WID),
                pltpu.VMEM((nz, 2 * rw, HD), BF),
                pltpu.VMEM((nz, 2 * rw, HD), BF),
                pltpu.VMEM((nz, 2 * rw, WID), BF),
                pltpu.VMEM((nz, 2 * rw, WID), BF),
                pltpu.SemaphoreType.DMA((9,)),
                pltpu.SemaphoreType.DMA((copies,)),
                pltpu.SemaphoreType.DMA((copies,)),
            ],
            compiler_params=pltpu.CompilerParams(
                collective_id=0, has_side_effects=True, vmem_limit_bytes=48 * 1024 * 1024
            ),
            cost_estimate=pl.CostEstimate(
                flops=1_600_000_000, bytes_accessed=3_000_000, transcendentals=300_000
            ),
        )(pt, mo, gm, gp, wq, wk, wv, rf, ids)

    stream = P("dp", "seq", "head")
    return jax.shard_map(
        shards,
        mesh=mesh,
        in_specs=(
            stream,
            stream,
            stream,
            stream,
            P(None, "head"),
            P(None, "head"),
            P(None, "head"),
            P("head", None, None),
            P("dp", "seq"),
        ),
        out_specs=(
            stream,
            stream,
            P(("seq", "dp"), "head"),
            P(("seq", "dp"), "head"),
            P(("seq", "dp"), "head"),
        ),
        check_vma=False,
    )
```

```python
import functools

import jax
import jax.numpy as jnp
from jax import lax
from jax.experimental import pallas as pl
from jax.experimental.pallas import tpu as pltpu
from jax.sharding import PartitionSpec as P

MESH = pl.DeviceIdType.MESH
BF = jnp.bfloat16
F32 = jnp.float32
EPSILON = 1e-06
TOK = 256
D = 1024
WID = 256
HD = 128
FEAT = 256
IDR = 16
PIECES = 2
CUT = FEAT // PIECES
MSG = CUT + IDR
NX = 4


def nn(a, b):
    return jnp.dot(a, b, preferred_element_type=F32)


def nt(a, b):
    return lax.dot_general(a, b, (((1,), (1,)), ((), ())), preferred_element_type=F32)


def tn(a, b):
    return lax.dot_general(a, b, (((0,), (0,)), ((), ())), preferred_element_type=F32)


def kernel(
    nz,
    ny,
    grad_scale,
    pt_h,
    mo_h,
    gm_h,
    gp_h,
    wq_h,
    wk_h,
    wv_h,
    rf_h,
    ids_h,
    fi_o,
    gs_o,
    wg_o,
    xs,
    moh,
    gmh,
    gp,
    w3,
    wkv,
    wqc,
    rf,
    ids,
    nrm,
    ntp,
    qb,
    kb,
    vb,
    fq,
    fk,
    pair,
    dpr,
    ga,
    dfk,
    dvl,
    dh,
    fib,
    fic,
    gsb,
    wgb,
    fmsg,
    fgot,
    ftwo,
    fst,
    bmsg,
    bgot,
    btwo,
    bst,
    xso,
    xsm,
    xro,
    xrm,
    dots,
    dotr,
    yso,
    ysm,
    yro,
    yrm,
    zs,
    zr,
    lsem,
    osem,
    ssem,
    rsem,
):
    seq = lax.axis_index("seq")
    x = lax.axis_index("head")
    y = lax.axis_index("dp")
    z = seq // 2
    c = seq % 2
    oc = 1 - c
    rw = D // (2 * nz * ny)
    right = lax.rem(x + 1, NX)
    left = lax.rem(x + NX - 1, NX)
    opp = lax.rem(x + 2, NX)
    up, down = lax.rem(y + 1, ny), lax.rem(y + ny - 1, ny)

    def at_x(other):
        return (seq, other, y)

    def at_y(other):
        return (seq, x, other)

    def at_z(step):
        return (lax.rem(z + step + nz, nz) * 2 + c, x, y)

    sibling = (z * 2 + oc, x, y)

    barrier = pltpu.get_barrier_semaphore()
    peers = [at_x(lax.rem(x + d, NX)) for d in range(1, NX)]
    peers += [sibling]
    peers += [at_z(d) for d in range(1, nz)]
    peers += [at_y(lax.rem(y + d, ny)) for d in range(1, ny)]
    for peer in peers:
        pl.semaphore_signal(barrier, inc=1, device_id=peer, device_id_type=MESH)

    mine = pl.ds(pl.multiple_of(c * HD, HD), HD)
    others = pl.ds(pl.multiple_of(oc * HD, HD), HD)
    local = {}
    for i, (name, src, dst) in enumerate(
        [
            ("pt", pt_h.at[0], xs.at[c, 0]),
            ("ids", ids_h, ids.at[c]),
            ("wk", wk_h.at[:, mine], wkv.at[:, pl.ds(0, HD)]),
            ("wv", wv_h.at[:, mine], wkv.at[:, pl.ds(HD, HD)]),
            ("rf", rf_h.at[c], rf),
            ("wq", wq_h.at[:, mine], wqc),
            ("gm", gm_h.at[0, :, mine], gmh.at[c]),
            ("mo", mo_h.at[0, :, mine], moh.at[c]),
            ("w0", wq_h, w3.at[0]),
            ("w1", wk_h, w3.at[1]),
            ("w2", wv_h, w3.at[2]),
            ("gp", gp_h.at[0], gp),
        ]
    ):
        local[name] = pltpu.make_async_copy(src, dst, lsem.at[i])
        local[name].start()

    counter = [0]
    pending = []

    def send(src, dst, device):
        i = counter[0]
        counter[0] += 1
        copy = pltpu.make_async_remote_copy(
            src_ref=src,
            dst_ref=dst,
            send_sem=ssem.at[i],
            recv_sem=rsem.at[i],
            device_id=device,
            device_id_type=MESH,
        )
        copy.start()
        pending.append(copy)
        return copy

    pl.semaphore_wait(barrier, len(peers))

    top, bot = pl.ds(0, TOK // 2), pl.ds(TOK // 2, TOK // 2)
    l_top = send(pt_h.at[0, top], xs.at[c, 1, top], at_x(right))
    r_bot = send(pt_h.at[0, bot], xs.at[c, 3, bot], at_x(left))
    l_bot = send(pt_h.at[0, bot], xs.at[c, 1, bot], at_x(right))
    r_top = send(pt_h.at[0, top], xs.at[c, 3, top], at_x(left))
    passed = [send(pt_h.at[0], xs.at[c, 0], sibling)]
    c_ids = send(ids_h, ids.at[c], sibling)
    c_gm = send(gm_h.at[0, :, others], gmh.at[c], sibling)
    c_mo = send(mo_h.at[0, :, others], moh.at[c], sibling)

    def pass_on(slot, rows):
        passed.append(send(xs.at[c, slot, rows], xs.at[c, slot, rows], sibling))

    l_top.wait_recv()
    o_top = send(xs.at[c, 1, top], xs.at[c, 2, top], at_x(right))
    pass_on(1, top)
    r_bot.wait_recv()
    o_bot = send(xs.at[c, 3, bot], xs.at[c, 2, bot], at_x(left))
    pass_on(3, bot)

    local["ids"].wait()
    c_ids.wait_recv()
    row_ids, col_ids = [], []
    for b in range(2):
        row_ids.append(jnp.broadcast_to(ids[b].astype(F32), (TOK, TOK)))
        col_ids.append(row_ids[b].T)
    tri = lax.broadcasted_iota(jnp.int32, (TOK, TOK), 0) >= lax.broadcasted_iota(
        jnp.int32, (TOK, TOK), 1
    )
    chip_last = row_ids[1][:, TOK - 1 : TOK]
    chip_first = row_ids[0][:, 0:1]
    last_rows = jnp.broadcast_to(chip_last[:IDR], (IDR, HD)).astype(BF)
    first_rows = jnp.broadcast_to(chip_first[:IDR], (IDR, HD)).astype(BF)
    for i in range(PIECES):
        fmsg[i, CUT:MSG] = last_rows
        bmsg[i, CUT:MSG] = first_rows

    def on_rows(b, ident):
        return col_ids[b][:, :HD] == ident

    def square_sum(b, slot):
        wide = xs[b, slot].astype(F32)
        return jnp.sum(wide * wide, axis=1, keepdims=True)

    def normalize(b, squares):
        inv = lax.rsqrt(squares * (1.0 / D) + EPSILON)
        for slot in range(NX):
            nrm[b, slot] = (xs[b, slot].astype(F32) * inv).astype(BF)
        return inv

    def source(slot):
        return lax.rem(x + NX - slot, NX)

    def project(b, weights):
        total = None
        for slot in range(NX):
            rows = pl.ds(pl.multiple_of(source(slot) * WID, WID), WID)
            term = nn(nrm[b, slot], weights[rows, :])
            total = term if total is None else total + term
        return total.astype(BF)

    def features(projected):
        wide = projected.astype(F32)
        norm = jnp.sum(wide * wide, axis=1, keepdims=True)
        exponent = nn(projected, rf[...]) * (1.0 / HD**0.25) - norm * (1.0 / (2.0 * HD**0.5))
        return (jnp.exp(exponent) * (1.0 / FEAT**0.5)).astype(BF)

    def keys_values(b):
        both = project(b, wkv)
        kb[b] = both[:, :HD]
        vb[b] = both[:, HD:]
        fk[b] = features(both[:, :HD])

    local["pt"].wait()
    squares = square_sum(c, 0)
    l_bot.wait_recv()
    pass_on(1, bot)
    r_top.wait_recv()
    pass_on(3, top)
    squares = squares + square_sum(c, 1) + square_sum(c, 3)
    o_top.wait_recv()
    pass_on(2, top)
    o_bot.wait_recv()
    pass_on(2, bot)
    squares = squares + square_sum(c, 2)
    inv_rms = normalize(c, squares)
    local["wk"].wait()
    local["wv"].wait()
    local["rf"].wait()
    keys_values(c)
    for copy in passed:
        copy.wait_recv()
    squares = square_sum(oc, 0) + square_sum(oc, 1) + square_sum(oc, 3) + square_sum(oc, 2)
    normalize(oc, squares)
    keys_values(oc)

    def outer_sum(left_ref, right_ref, ident):
        total = None
        for b in range(2):
            masked = jnp.where(on_rows(b, ident), right_ref[b].astype(F32), 0.0).astype(BF)
            term = tn(left_ref[b], masked)
            total = term if total is None else total + term
        return total.astype(BF)

    def merge(near, far):
        return near[:CUT] + jnp.where(near[CUT : CUT + 1] == far[CUT : CUT + 1], far[:CUT], 0.0)

    class Scan:
        def __init__(self, sign, msg, got, two, state):
            self.sign, self.msg, self.got, self.two, self.state = sign, msg, got, two, state

        def begin(self, outer):
            self.near, self.far = [], []
            for i in range(PIECES):
                self.msg[i, 0:CUT] = outer[i * CUT : (i + 1) * CUT]
                self.near.append(send(self.msg.at[i], self.got.at[0, i], at_z(self.sign)))
                self.far.append(send(self.msg.at[i], self.got.at[1, i], at_z(2 * self.sign)))

        def pairs(self):
            self.last = []
            for i in range(PIECES):
                self.near[i].wait_recv()
                self.far[i].wait_recv()
                near, far = self.got[0, i].astype(F32), self.got[1, i].astype(F32)
                self.two[i, 0:CUT] = merge(near, far).astype(BF)
                self.two[i, CUT:MSG] = self.got[0, i, CUT:MSG]
                self.last.append(send(self.two.at[i], self.got.at[2, i], at_z(2 * self.sign)))

        def finish(self):
            for i in range(PIECES):
                self.last[i].wait_recv()
                near, far = self.two[i].astype(F32), self.got[2, i].astype(F32)
                self.state[i * CUT : (i + 1) * CUT] = merge(near, far).astype(BF)
            return self.two[0, CUT : CUT + 1].astype(F32)

    forward = Scan(1, fmsg, fgot, ftwo, fst)
    forward.begin(outer_sum(fk, vb, chip_last))

    local["wq"].wait()
    for b in range(2):
        qb[b] = project(b, wqc)
        fq[b] = features(qb[b])

    forward.pairs()

    blocks = [(0, 0), (1, 0), (1, 1)]
    allowed = []
    for i, (b, s) in enumerate(blocks):
        same = row_ids[s] == col_ids[b]
        allowed.append(same & tri if b == s else same)
        pair[i] = jnp.where(allowed[i], nt(fq[b], fk[s]), 0.0).astype(BF)
    attn = [nn(pair[0], vb[0]), nn(pair[1], vb[0]) + nn(pair[2], vb[1])]

    per_slot = nz // NX
    for slot in range(NX):
        place = pl.ds(pl.multiple_of(source(slot) * (per_slot * rw), per_slot * rw), per_slot * rw)
        for b in range(2):
            turned = nrm[b, slot].astype(F32).T.reshape(per_slot, 2, ny, rw, TOK)
            turned = jnp.where(c == 0, turned[:, 0], turned[:, 1])
            for part in range(ny):
                block = turned[:, part].reshape(per_slot * rw, TOK)
                ntp[part, place, b * TOK : (b + 1) * TOK] = block.astype(BF)

    local["gm"].wait()
    local["mo"].wait()
    c_gm.wait_recv()
    c_mo.wait_recv()
    f_id = forward.finish()

    acts = []
    for b in range(2):
        attention = attn[b] + jnp.where(on_rows(b, f_id), nn(fq[b], fst[...]), 0.0)
        inv_attn = lax.rsqrt(jnp.mean(attention * attention, axis=1, keepdims=True) + EPSILON)
        act = attention * inv_attn
        acts.append(act)
        grad_act = gmh[b].astype(F32)
        inner = jnp.mean(grad_act * act, axis=1, keepdims=True)
        ga[b] = (inv_attn * (grad_act - act * inner)).astype(BF)

    backward = Scan(-1, bmsg, bgot, btwo, bst)
    backward.begin(outer_sum(fq, ga, chip_first))

    for b in range(2):
        fib[b] = (moh[b].astype(F32) - acts[b]).astype(BF)
    c_fi = send(fib.at[oc], fic, sibling)
    out_fi = pltpu.make_async_copy(fib.at[c], fi_o.at[0, :, mine], osem.at[0])
    out_fi.start()

    def feature_grad(dfeature, feature, projected):
        dexponent = dfeature * feature.astype(F32)
        back = nt(dexponent.astype(BF), rf[...])
        totals = jnp.sum(dexponent, axis=1, keepdims=True)
        result = back * (1.0 / HD**0.25) - projected.astype(F32) * (totals * (1.0 / HD**0.5))
        return result.astype(BF)

    for i, (b, s) in enumerate(blocks):
        dpr[i] = jnp.where(allowed[i], nt(ga[b], vb[s]), 0.0).astype(BF)
    dfq = [nn(dpr[0], fk[0]), nn(dpr[1], fk[0]) + nn(dpr[2], fk[1])]

    backward.pairs()

    for b in range(2):
        masked = jnp.where(on_rows(b, f_id), ga[b].astype(F32), 0.0).astype(BF)
        dfeat = dfq[b] + nt(masked, fst[...])
        dh[0, b * TOK : (b + 1) * TOK, mine] = feature_grad(dfeat, fq[b], qb[b])
    c_dq = send(dh.at[0, :, mine], dh.at[0, :, mine], sibling)

    dfk[0] = tn(dpr[0], fq[0]) + tn(dpr[1], fq[1])
    dfk[1] = tn(dpr[2], fq[1])
    dvl[0] = tn(pair[0], ga[0]) + tn(pair[1], ga[1])
    dvl[1] = tn(pair[2], ga[1])

    class Ring:
        def __init__(self, so, sm, ro, rm, to_right, to_left):
            self.so, self.sm, self.ro, self.rm = so, sm, ro, rm
            self.to_right, self.to_left = to_right, to_left
            self.half = so.shape[1]

        def opposite(self, block):
            self.so[0] = block[: self.half].astype(BF)
            self.o0 = send(self.so.at[0], self.ro.at[0], self.to_right)
            self.so[1] = block[self.half :].astype(BF)
            self.o1 = send(self.so.at[1], self.ro.at[1], self.to_left)

        def sides(self, to_right, to_left):
            self.sm[0, 1] = to_right[self.half :].astype(BF)
            self.m01 = send(self.sm.at[0, 1], self.rm.at[0, 1], self.to_right)
            self.sm[1, 0] = to_left[: self.half].astype(BF)
            self.m10 = send(self.sm.at[1, 0], self.rm.at[1, 0], self.to_left)
            self.r_top = to_right[: self.half]
            self.l_bot = to_left[self.half :]

        def relay(self):
            self.o0.wait_recv()
            self.sm[0, 0] = (self.r_top + self.ro[0].astype(F32)).astype(BF)
            self.m00 = send(self.sm.at[0, 0], self.rm.at[0, 0], self.to_right)
            self.o1.wait_recv()
            self.sm[1, 1] = (self.l_bot + self.ro[1].astype(F32)).astype(BF)
            self.m11 = send(self.sm.at[1, 1], self.rm.at[1, 1], self.to_left)

        def total(self, own):
            for copy in (self.m01, self.m10, self.m00, self.m11):
                copy.wait_recv()
            halves = [
                own[i * self.half : (i + 1) * self.half]
                + self.rm[0, i].astype(F32)
                + self.rm[1, i].astype(F32)
                for i in range(2)
            ]
            return jnp.concatenate(halves, axis=0)

    def y_ring(which):
        return Ring(yso.at[which], ysm.at[which], yro.at[which], yrm.at[which], at_y(up), at_y(down))

    def weight_rows(which, part):
        return nn(ntp[part], dh[which]) * grad_scale

    def start_weights(which):
        ring = y_ring(which)
        ring.opposite(weight_rows(which, lax.rem(y + 2, ny)))
        ring.sides(weight_rows(which, up), weight_rows(which, down))
        return ring

    def z_send(which, total):
        split = total.reshape(nz, rw, WID)
        zs[which] = jnp.concatenate([split[:, :, :HD], split[:, :, HD:]], axis=1).astype(BF)
        copies = []
        for d in range(1, nz):
            to = lax.rem(z + d, nz)
            copies.append(send(zs.at[which, to], zr.at[which, d], at_z(d)))
        return copies

    def z_total(which, copies):
        total = zs[which, z].astype(F32)
        for d in range(1, nz):
            copies[d - 1].wait_recv()
            total = total + zr[which, d].astype(F32)
        wgb[which] = jnp.concatenate([total[:rw], total[rw:]], axis=1)

    c_dq.wait_recv()
    ring_q = start_weights(0)
    own_q = weight_rows(0, y)

    b_id = backward.finish()

    for b in range(2):
        carried = jnp.where(on_rows(b, b_id), nn(fk[b], bst[...]), 0.0)
        dh[2, b * TOK : (b + 1) * TOK, mine] = (dvl[b] + carried).astype(BF)
    c_dv = send(dh.at[2, :, mine], dh.at[2, :, mine], sibling)
    for b in range(2):
        masked = jnp.where(on_rows(b, b_id), vb[b].astype(F32), 0.0).astype(BF)
        dfeat = dfk[b] + nt(masked, bst[...])
        dh[1, b * TOK : (b + 1) * TOK, mine] = feature_grad(dfeat, fk[b], kb[b])
    c_dk = send(dh.at[1, :, mine], dh.at[1, :, mine], sibling)
    ring_q.relay()
    local["w0"].wait()
    local["w1"].wait()
    local["w2"].wait()

    c_dv.wait_recv()
    ring_v = start_weights(2)
    c_dk.wait_recv()
    ring_k = start_weights(1)

    own_rows = pl.ds(pl.multiple_of(c * TOK, TOK), TOK)

    def normed_term(owner, slot):
        rows = pl.ds(pl.multiple_of(owner * WID, WID), WID)
        term = nt(dh[0, own_rows, :], w3[0, rows, :])
        term = term + nt(dh[1, own_rows, :], w3[1, rows, :])
        term = term + nt(dh[2, own_rows, :], w3[2, rows, :])
        return term, jnp.sum(term * xs[c, slot].astype(F32), axis=1, keepdims=True)

    ring_x = Ring(xso, xsm, xro, xrm, at_x(right), at_x(left))
    term, dot = normed_term(opp, 2)
    ring_x.opposite(term)
    term_r, dot_r = normed_term(right, 3)
    term_l, dot_l = normed_term(left, 1)
    ring_x.sides(term_r, term_l)

    ring_v.relay()
    z_q = z_send(0, ring_q.total(own_q))
    ring_k.relay()
    ring_x.relay()

    term_own, dot_own = normed_term(x, 0)
    dot = (dot + dot_r + dot_l + dot_own) * inv_rms
    dots[...] = jnp.broadcast_to(dot, (TOK, HD)).T[:8]
    c_dot = [send(dots, dotr.at[d - 1], at_x(lax.rem(x + d, NX))) for d in range(1, NX)]
    own_v = weight_rows(2, y)
    own_k = weight_rows(1, y)

    z_v = z_send(2, ring_v.total(own_v))
    z_k = z_send(1, ring_k.total(own_k))

    for copy in c_dot:
        copy.wait_recv()
    dot_rows = dots[...] + dotr[0] + dotr[1] + dotr[2]
    dot_all = jnp.broadcast_to(dot_rows[0:1], (HD, TOK)).T
    local["gp"].wait()
    grad_normed = ring_x.total(term_own)
    norm_own = xs[c, 0].astype(F32) * inv_rms
    mean = dot_all[:, 0:1] * (1.0 / D)
    gsb[...] = (gp[...].astype(F32) + inv_rms * (grad_normed - norm_own * mean)).astype(BF)
    out_gs = pltpu.make_async_copy(gsb, gs_o.at[0], osem.at[1])
    out_gs.start()
    c_fi.wait_recv()
    out_fi2 = pltpu.make_async_copy(fic, fi_o.at[0, :, others], osem.at[2])
    out_fi2.start()

    z_total(0, z_q)
    z_total(2, z_v)
    z_total(1, z_k)
    out_wg = pltpu.make_async_copy(wgb, wg_o, osem.at[3])
    out_wg.start()
    for copy in (out_fi, out_gs, out_fi2, out_wg):
        copy.wait()
    for copy in pending:
        copy.wait_send()


def hand_out(fi, gs, wg, fi_o, gs_o, q_o, k_o, v_o, sem):
    copies = [
        pltpu.make_async_copy(src, dst, sem.at[i])
        for i, (src, dst) in enumerate(
            [(fi, fi_o), (gs, gs_o), (wg.at[0], q_o), (wg.at[1], k_o), (wg.at[2], v_o)]
        )
    ]
    for copy in copies:
        copy.start()
    for copy in copies:
        copy.wait()


def solution(mesh):
    nz = mesh.shape["seq"] // 2
    ny = mesh.shape["dp"]
    rw = D // (2 * nz * ny)
    rows_y = nz * rw
    half = rows_y // 2

    scan = [
        pltpu.VMEM((PIECES, MSG, HD), BF),
        pltpu.VMEM((3, PIECES, MSG, HD), BF),
        pltpu.VMEM((PIECES, MSG, HD), BF),
        pltpu.VMEM((FEAT, HD), BF),
    ]

    def shards(pt, mo, gm, gp, wq, wk, wv, rf, ids):
        total_rows = TOK * 2 * nz * ny
        copies = 110
        stream = jax.ShapeDtypeStruct((1, TOK, WID), BF)
        grads = jax.ShapeDtypeStruct((rw, WID), F32)
        limit = pltpu.CompilerParams(
            collective_id=0, has_side_effects=True, vmem_limit_bytes=58 * 1024 * 1024
        )
        first_in, grad_second, weights = pl.pallas_call(
            functools.partial(kernel, nz, ny, 1.0 / total_rows**0.5),
            out_shape=(stream, stream, jax.ShapeDtypeStruct((3, rw, WID), F32)),
            in_specs=[pl.BlockSpec(memory_space=pl.ANY)] * 9,
            out_specs=[pl.BlockSpec(memory_space=pl.ANY)] * 3,
            scratch_shapes=[
                pltpu.VMEM((2, NX, TOK, WID), BF),
                pltpu.VMEM((2, TOK, HD), BF),
                pltpu.VMEM((2, TOK, HD), BF),
                pltpu.VMEM((TOK, WID), BF),
                pltpu.VMEM((3, D, WID), BF),
                pltpu.VMEM((D, WID), BF),
                pltpu.VMEM((D, HD), BF),
                pltpu.VMEM((HD, FEAT), BF),
                pltpu.VMEM((2, 1, TOK), jnp.int32),
                pltpu.VMEM((2, NX, TOK, WID), BF),
                pltpu.VMEM((ny, rows_y, 2 * TOK), BF),
                pltpu.VMEM((2, TOK, HD), BF),
                pltpu.VMEM((2, TOK, HD), BF),
                pltpu.VMEM((2, TOK, HD), BF),
                pltpu.VMEM((2, TOK, FEAT), BF),
                pltpu.VMEM((2, TOK, FEAT), BF),
                pltpu.VMEM((3, TOK, TOK), BF),
                pltpu.VMEM((3, TOK, TOK), BF),
                pltpu.VMEM((2, TOK, HD), BF),
                pltpu.VMEM((2, TOK, FEAT), F32),
                pltpu.VMEM((2, TOK, HD), F32),
                pltpu.VMEM((3, 2 * TOK, WID), BF),
                pltpu.VMEM((2, TOK, HD), BF),
                pltpu.VMEM((TOK, HD), BF),
                pltpu.VMEM((TOK, WID), BF),
                pltpu.VMEM((3, rw, WID), F32),
                *scan,
                *scan,
                pltpu.VMEM((2, TOK // 2, WID), BF),
                pltpu.VMEM((2, 2, TOK // 2, WID), BF),
                pltpu.VMEM((2, TOK // 2, WID), BF),
                pltpu.VMEM((2, 2, TOK // 2, WID), BF),
                pltpu.VMEM((8, TOK), F32),
                pltpu.VMEM((NX - 1, 8, TOK), F32),
                pltpu.VMEM((3, 2, half, WID), BF),
                pltpu.VMEM((3, 2, 2, half, WID), BF),
                pltpu.VMEM((3, 2, half, WID), BF),
                pltpu.VMEM((3, 2, 2, half, WID), BF),
                pltpu.VMEM((3, nz, 2 * rw, HD), BF),
                pltpu.VMEM((3, nz, 2 * rw, HD), BF),
                pltpu.SemaphoreType.DMA((12,)),
                pltpu.SemaphoreType.DMA((4,)),
                pltpu.SemaphoreType.DMA((copies,)),
                pltpu.SemaphoreType.DMA((copies,)),
            ],
            compiler_params=limit,
            cost_estimate=pl.CostEstimate(
                flops=1_800_000_000, bytes_accessed=4_000_000, transcendentals=300_000
            ),
        )(pt, mo, gm, gp, wq, wk, wv, rf, ids)
        return pl.pallas_call(
            hand_out,
            out_shape=(stream, stream, grads, grads, grads),
            in_specs=[pl.BlockSpec(memory_space=pl.ANY)] * 3,
            out_specs=[pl.BlockSpec(memory_space=pl.ANY)] * 5,
            scratch_shapes=[pltpu.SemaphoreType.DMA((5,))],
            compiler_params=pltpu.CompilerParams(vmem_limit_bytes=58 * 1024 * 1024),
        )(first_in, grad_second, weights)

    stream = P("dp", "seq", "head")
    return jax.shard_map(
        shards,
        mesh=mesh,
        in_specs=(
            stream,
            stream,
            stream,
            stream,
            P(None, "head"),
            P(None, "head"),
            P(None, "head"),
            P("head", None, None),
            P("dp", "seq"),
        ),
        out_specs=(
            stream,
            stream,
            P(("seq", "dp"), "head"),
            P(("seq", "dp"), "head"),
            P(("seq", "dp"), "head"),
        ),
        check_vma=False,
    )
```

```python
import functools

import jax
import jax.numpy as jnp
from jax import lax
from jax.experimental import pallas as pl
from jax.experimental.pallas import tpu as pltpu
from jax.sharding import PartitionSpec as P

MESH = pl.DeviceIdType.MESH
BF = jnp.bfloat16
F32 = jnp.float32
EPSILON = 1e-06
TOK = 256
D = 1024
WID = 256
HD = 128
FEAT = 256
IDR = 16
PIECES = 2
CUT = FEAT // PIECES
MSG = CUT + IDR
NX = 4


def nn(a, b):
    return jnp.dot(a, b, preferred_element_type=F32)


def nt(a, b):
    return lax.dot_general(a, b, (((1,), (1,)), ((), ())), preferred_element_type=F32)


def tn(a, b):
    return lax.dot_general(a, b, (((0,), (0,)), ((), ())), preferred_element_type=F32)


def kernel(
    nz,
    ny,
    grad_scale,
    pt_h,
    mo_h,
    gm_h,
    gp_h,
    wq_h,
    wk_h,
    wv_h,
    rf_h,
    ids_h,
    fi_o,
    gs_o,
    wg_o,
    xs,
    moh,
    gmh,
    gp,
    w3,
    wkv,
    wqc,
    rf,
    ids,
    nrm,
    ntp,
    qb,
    kb,
    vb,
    fq,
    fk,
    pair,
    dpr,
    ga,
    dfk,
    dvl,
    dh,
    fib,
    fic,
    gsb,
    wgb,
    fmsg,
    fgot,
    ftwo,
    fst,
    bmsg,
    bgot,
    btwo,
    bst,
    xso,
    xsm,
    xro,
    xrm,
    dots,
    dotr,
    yso,
    ysm,
    yro,
    yrm,
    zs,
    zr,
    lsem,
    osem,
    ssem,
    rsem,
):
    seq = lax.axis_index("seq")
    x = lax.axis_index("head")
    y = lax.axis_index("dp")
    z = seq // 2
    c = seq % 2
    oc = 1 - c
    rw = D // (2 * nz * ny)
    right = lax.rem(x + 1, NX)
    left = lax.rem(x + NX - 1, NX)
    opp = lax.rem(x + 2, NX)
    up, down = lax.rem(y + 1, ny), lax.rem(y + ny - 1, ny)

    def at_x(other):
        return (seq, other, y)

    def at_y(other):
        return (seq, x, other)

    def at_z(step):
        return (lax.rem(z + step + nz, nz) * 2 + c, x, y)

    sibling = (z * 2 + oc, x, y)

    barrier = pltpu.get_barrier_semaphore()
    peers = [at_x(lax.rem(x + d, NX)) for d in range(1, NX)]
    peers += [sibling]
    peers += [at_z(d) for d in range(1, nz)]
    peers += [at_y(lax.rem(y + d, ny)) for d in range(1, ny)]
    for peer in peers:
        pl.semaphore_signal(barrier, inc=1, device_id=peer, device_id_type=MESH)

    mine = pl.ds(pl.multiple_of(c * HD, HD), HD)
    others = pl.ds(pl.multiple_of(oc * HD, HD), HD)
    local = {}
    for i, (name, src, dst) in enumerate(
        [
            ("pt", pt_h.at[0], xs.at[c, 0]),
            ("ids", ids_h, ids.at[c]),
            ("wk", wk_h.at[:, mine], wkv.at[:, pl.ds(0, HD)]),
            ("wv", wv_h.at[:, mine], wkv.at[:, pl.ds(HD, HD)]),
            ("rf", rf_h.at[c], rf),
            ("wq", wq_h.at[:, mine], wqc),
            ("gm", gm_h.at[0, :, mine], gmh.at[c]),
            ("mo", mo_h.at[0, :, mine], moh.at[c]),
            ("w0", wq_h, w3.at[0]),
            ("w1", wk_h, w3.at[1]),
            ("w2", wv_h, w3.at[2]),
            ("gp", gp_h.at[0], gp),
        ]
    ):
        local[name] = pltpu.make_async_copy(src, dst, lsem.at[i])

    counter = [0]
    pending = []

    def send(src, dst, device):
        i = counter[0]
        counter[0] += 1
        copy = pltpu.make_async_remote_copy(
            src_ref=src,
            dst_ref=dst,
            send_sem=ssem.at[i],
            recv_sem=rsem.at[i],
            device_id=device,
            device_id_type=MESH,
        )
        copy.start()
        pending.append(copy)
        return copy

    early = ("pt", "ids")
    for name in early:
        local[name].start()
    pl.semaphore_wait(barrier, len(peers))

    top, bot = pl.ds(0, TOK // 2), pl.ds(TOK // 2, TOK // 2)
    l_top = send(pt_h.at[0, top], xs.at[c, 1, top], at_x(right))
    r_bot = send(pt_h.at[0, bot], xs.at[c, 3, bot], at_x(left))
    l_bot = send(pt_h.at[0, bot], xs.at[c, 1, bot], at_x(right))
    r_top = send(pt_h.at[0, top], xs.at[c, 3, top], at_x(left))
    passed = [send(pt_h.at[0], xs.at[c, 0], sibling)]
    c_ids = send(ids_h, ids.at[c], sibling)
    for name, copy in local.items():
        if name not in early:
            copy.start()
    c_gm = send(gm_h.at[0, :, others], gmh.at[c], sibling)
    c_mo = send(mo_h.at[0, :, others], moh.at[c], sibling)

    def pass_on(slot, rows):
        passed.append(send(xs.at[c, slot, rows], xs.at[c, slot, rows], sibling))

    l_top.wait_recv()
    o_top = send(xs.at[c, 1, top], xs.at[c, 2, top], at_x(right))
    pass_on(1, top)
    r_bot.wait_recv()
    o_bot = send(xs.at[c, 3, bot], xs.at[c, 2, bot], at_x(left))
    pass_on(3, bot)

    local["ids"].wait()
    c_ids.wait_recv()
    row_ids, col_ids = [], []
    for b in range(2):
        row_ids.append(jnp.broadcast_to(ids[b].astype(F32), (TOK, TOK)))
        col_ids.append(row_ids[b].T)
    tri = lax.broadcasted_iota(jnp.int32, (TOK, TOK), 0) >= lax.broadcasted_iota(
        jnp.int32, (TOK, TOK), 1
    )
    chip_last = row_ids[1][:, TOK - 1 : TOK]
    chip_first = row_ids[0][:, 0:1]
    last_rows = jnp.broadcast_to(chip_last[:IDR], (IDR, HD)).astype(BF)
    first_rows = jnp.broadcast_to(chip_first[:IDR], (IDR, HD)).astype(BF)
    for i in range(PIECES):
        fmsg[i, CUT:MSG] = last_rows
        bmsg[i, CUT:MSG] = first_rows

    def on_rows(b, ident):
        return col_ids[b][:, :HD] == ident

    def square_sum(b, slot):
        wide = xs[b, slot].astype(F32)
        return jnp.sum(wide * wide, axis=1, keepdims=True)

    def normalize(b, squares):
        inv = lax.rsqrt(squares * (1.0 / D) + EPSILON)
        for slot in range(NX):
            nrm[b, slot] = (xs[b, slot].astype(F32) * inv).astype(BF)
        return inv

    def source(slot):
        return lax.rem(x + NX - slot, NX)

    def project(b, weights):
        total = None
        for slot in range(NX):
            rows = pl.ds(pl.multiple_of(source(slot) * WID, WID), WID)
            term = nn(nrm[b, slot], weights[rows, :])
            total = term if total is None else total + term
        return total.astype(BF)

    def features(projected):
        wide = projected.astype(F32)
        norm = jnp.sum(wide * wide, axis=1, keepdims=True)
        exponent = nn(projected, rf[...]) * (1.0 / HD**0.25) - norm * (1.0 / (2.0 * HD**0.5))
        return (jnp.exp(exponent) * (1.0 / FEAT**0.5)).astype(BF)

    def keys_values(b):
        both = project(b, wkv)
        kb[b] = both[:, :HD]
        vb[b] = both[:, HD:]
        fk[b] = features(both[:, :HD])

    local["pt"].wait()
    squares = square_sum(c, 0)
    l_bot.wait_recv()
    pass_on(1, bot)
    r_top.wait_recv()
    pass_on(3, top)
    squares = squares + square_sum(c, 1) + square_sum(c, 3)
    o_top.wait_recv()
    pass_on(2, top)
    o_bot.wait_recv()
    pass_on(2, bot)
    squares = squares + square_sum(c, 2)
    inv_rms = normalize(c, squares)
    local["wk"].wait()
    local["wv"].wait()
    local["rf"].wait()
    keys_values(c)
    for copy in passed:
        copy.wait_recv()
    squares = square_sum(oc, 0) + square_sum(oc, 1) + square_sum(oc, 3) + square_sum(oc, 2)
    normalize(oc, squares)
    keys_values(oc)

    def outer_sum(left_ref, right_ref, ident):
        total = None
        for b in range(2):
            masked = jnp.where(on_rows(b, ident), right_ref[b].astype(F32), 0.0).astype(BF)
            term = tn(left_ref[b], masked)
            total = term if total is None else total + term
        return total.astype(BF)

    def merge(near, far):
        return near[:CUT] + jnp.where(near[CUT : CUT + 1] == far[CUT : CUT + 1], far[:CUT], 0.0)

    class Scan:
        def __init__(self, sign, msg, got, two, state):
            self.sign, self.msg, self.got, self.two, self.state = sign, msg, got, two, state

        def begin(self, outer):
            self.near, self.far = [], []
            for i in range(PIECES):
                self.msg[i, 0:CUT] = outer[i * CUT : (i + 1) * CUT]
                self.near.append(send(self.msg.at[i], self.got.at[0, i], at_z(self.sign)))
                self.far.append(send(self.msg.at[i], self.got.at[1, i], at_z(2 * self.sign)))

        def pairs(self):
            self.last = []
            for i in range(PIECES):
                self.near[i].wait_recv()
                self.far[i].wait_recv()
                near, far = self.got[0, i].astype(F32), self.got[1, i].astype(F32)
                self.two[i, 0:CUT] = merge(near, far).astype(BF)
                self.two[i, CUT:MSG] = self.got[0, i, CUT:MSG]
                self.last.append(send(self.two.at[i], self.got.at[2, i], at_z(2 * self.sign)))

        def finish(self):
            for i in range(PIECES):
                self.last[i].wait_recv()
                near, far = self.two[i].astype(F32), self.got[2, i].astype(F32)
                self.state[i * CUT : (i + 1) * CUT] = merge(near, far).astype(BF)
            return self.two[0, CUT : CUT + 1].astype(F32)

    forward = Scan(1, fmsg, fgot, ftwo, fst)
    forward.begin(outer_sum(fk, vb, chip_last))

    local["wq"].wait()
    for b in range(2):
        qb[b] = project(b, wqc)
        fq[b] = features(qb[b])

    forward.pairs()

    blocks = [(0, 0), (1, 0), (1, 1)]
    allowed = []
    for i, (b, s) in enumerate(blocks):
        same = row_ids[s] == col_ids[b]
        allowed.append(same & tri if b == s else same)
        pair[i] = jnp.where(allowed[i], nt(fq[b], fk[s]), 0.0).astype(BF)
    attn = [nn(pair[0], vb[0]), nn(pair[1], vb[0]) + nn(pair[2], vb[1])]

    per_slot = nz // NX
    for slot in range(NX):
        place = pl.ds(pl.multiple_of(source(slot) * (per_slot * rw), per_slot * rw), per_slot * rw)
        for b in range(2):
            turned = nrm[b, slot].astype(F32).T.reshape(per_slot, 2, ny, rw, TOK)
            turned = jnp.where(c == 0, turned[:, 0], turned[:, 1])
            for part in range(ny):
                block = turned[:, part].reshape(per_slot * rw, TOK)
                ntp[part, place, b * TOK : (b + 1) * TOK] = block.astype(BF)

    local["gm"].wait()
    local["mo"].wait()
    c_gm.wait_recv()
    c_mo.wait_recv()
    f_id = forward.finish()

    acts = []
    for b in range(2):
        attention = attn[b] + jnp.where(on_rows(b, f_id), nn(fq[b], fst[...]), 0.0)
        inv_attn = lax.rsqrt(jnp.mean(attention * attention, axis=1, keepdims=True) + EPSILON)
        act = attention * inv_attn
        acts.append(act)
        grad_act = gmh[b].astype(F32)
        inner = jnp.mean(grad_act * act, axis=1, keepdims=True)
        ga[b] = (inv_attn * (grad_act - act * inner)).astype(BF)

    backward = Scan(-1, bmsg, bgot, btwo, bst)
    backward.begin(outer_sum(fq, ga, chip_first))

    def feature_grad(dfeature, feature, projected):
        dexponent = dfeature * feature.astype(F32)
        back = nt(dexponent.astype(BF), rf[...])
        totals = jnp.sum(dexponent, axis=1, keepdims=True)
        result = back * (1.0 / HD**0.25) - projected.astype(F32) * (totals * (1.0 / HD**0.5))
        return result.astype(BF)

    for i, (b, s) in enumerate(blocks):
        dpr[i] = jnp.where(allowed[i], nt(ga[b], vb[s]), 0.0).astype(BF)
    dfq = [nn(dpr[0], fk[0]), nn(dpr[1], fk[0]) + nn(dpr[2], fk[1])]

    for b in range(2):
        masked = jnp.where(on_rows(b, f_id), ga[b].astype(F32), 0.0).astype(BF)
        dfeat = dfq[b] + nt(masked, fst[...])
        dh[0, b * TOK : (b + 1) * TOK, mine] = feature_grad(dfeat, fq[b], qb[b])
    c_dq = send(dh.at[0, :, mine], dh.at[0, :, mine], sibling)

    dfk[0] = tn(dpr[0], fq[0]) + tn(dpr[1], fq[1])
    dfk[1] = tn(dpr[2], fq[1])
    dvl[0] = tn(pair[0], ga[0]) + tn(pair[1], ga[1])
    dvl[1] = tn(pair[2], ga[1])

    backward.pairs()

    class Ring:
        def __init__(self, so, sm, ro, rm, to_right, to_left):
            self.so, self.sm, self.ro, self.rm = so, sm, ro, rm
            self.to_right, self.to_left = to_right, to_left
            self.half = so.shape[1]

        def opposite(self, block):
            self.so[0] = block[: self.half].astype(BF)
            self.o0 = send(self.so.at[0], self.ro.at[0], self.to_right)
            self.so[1] = block[self.half :].astype(BF)
            self.o1 = send(self.so.at[1], self.ro.at[1], self.to_left)

        def sides(self, to_right, to_left):
            self.sm[0, 1] = to_right[self.half :].astype(BF)
            self.m01 = send(self.sm.at[0, 1], self.rm.at[0, 1], self.to_right)
            self.sm[1, 0] = to_left[: self.half].astype(BF)
            self.m10 = send(self.sm.at[1, 0], self.rm.at[1, 0], self.to_left)
            self.r_top = to_right[: self.half]
            self.l_bot = to_left[self.half :]

        def relay(self):
            self.o0.wait_recv()
            self.sm[0, 0] = (self.r_top + self.ro[0].astype(F32)).astype(BF)
            self.m00 = send(self.sm.at[0, 0], self.rm.at[0, 0], self.to_right)
            self.o1.wait_recv()
            self.sm[1, 1] = (self.l_bot + self.ro[1].astype(F32)).astype(BF)
            self.m11 = send(self.sm.at[1, 1], self.rm.at[1, 1], self.to_left)

        def total(self, own):
            for copy in (self.m01, self.m10, self.m00, self.m11):
                copy.wait_recv()
            halves = [
                own[i * self.half : (i + 1) * self.half]
                + self.rm[0, i].astype(F32)
                + self.rm[1, i].astype(F32)
                for i in range(2)
            ]
            return jnp.concatenate(halves, axis=0)

    def y_ring(which):
        return Ring(yso.at[which], ysm.at[which], yro.at[which], yrm.at[which], at_y(up), at_y(down))

    def weight_rows(which, part):
        return nn(ntp[part], dh[which]) * grad_scale

    def start_weights(which):
        ring = y_ring(which)
        ring.opposite(weight_rows(which, lax.rem(y + 2, ny)))
        ring.sides(weight_rows(which, up), weight_rows(which, down))
        return ring

    def z_send(which, total):
        split = total.reshape(nz, rw, WID)
        zs[which] = jnp.concatenate([split[:, :, :HD], split[:, :, HD:]], axis=1).astype(BF)
        copies = []
        for d in range(1, nz):
            to = lax.rem(z + d, nz)
            copies.append(send(zs.at[which, to], zr.at[which, d], at_z(d)))
        return copies

    def z_total(which, copies):
        total = zs[which, z].astype(F32)
        for d in range(1, nz):
            copies[d - 1].wait_recv()
            total = total + zr[which, d].astype(F32)
        wgb[which] = jnp.concatenate([total[:rw], total[rw:]], axis=1)

    c_dq.wait_recv()
    ring_q = start_weights(0)

    for b in range(2):
        fib[b] = (moh[b].astype(F32) - acts[b]).astype(BF)
    c_fi = send(fib.at[oc], fic, sibling)
    out_fi = pltpu.make_async_copy(fib.at[c], fi_o.at[0, :, mine], osem.at[0])
    out_fi.start()

    own_q = weight_rows(0, y)
    ring_q.relay()

    b_id = backward.finish()

    for b in range(2):
        carried = jnp.where(on_rows(b, b_id), nn(fk[b], bst[...]), 0.0)
        dh[2, b * TOK : (b + 1) * TOK, mine] = (dvl[b] + carried).astype(BF)
    c_dv = send(dh.at[2, :, mine], dh.at[2, :, mine], sibling)
    for b in range(2):
        masked = jnp.where(on_rows(b, b_id), vb[b].astype(F32), 0.0).astype(BF)
        dfeat = dfk[b] + nt(masked, bst[...])
        dh[1, b * TOK : (b + 1) * TOK, mine] = feature_grad(dfeat, fk[b], kb[b])
    c_dk = send(dh.at[1, :, mine], dh.at[1, :, mine], sibling)
    z_q = z_send(0, ring_q.total(own_q))
    local["w0"].wait()
    local["w1"].wait()
    local["w2"].wait()

    c_dv.wait_recv()
    ring_v = start_weights(2)
    c_dk.wait_recv()
    ring_k = start_weights(1)

    own_rows = pl.ds(pl.multiple_of(c * TOK, TOK), TOK)

    def normed_term(owner, slot):
        rows = pl.ds(pl.multiple_of(owner * WID, WID), WID)
        term = nt(dh[0, own_rows, :], w3[0, rows, :])
        term = term + nt(dh[1, own_rows, :], w3[1, rows, :])
        term = term + nt(dh[2, own_rows, :], w3[2, rows, :])
        return term, jnp.sum(term * xs[c, slot].astype(F32), axis=1, keepdims=True)

    ring_x = Ring(xso, xsm, xro, xrm, at_x(right), at_x(left))
    term, dot = normed_term(opp, 2)
    ring_x.opposite(term)
    term_r, dot_r = normed_term(right, 3)
    term_l, dot_l = normed_term(left, 1)
    ring_x.sides(term_r, term_l)

    ring_v.relay()
    ring_k.relay()
    ring_x.relay()

    term_own, dot_own = normed_term(x, 0)
    dot = (dot + dot_r + dot_l + dot_own) * inv_rms
    dots[...] = jnp.broadcast_to(dot, (TOK, HD)).T[:8]
    c_dot = [send(dots, dotr.at[d - 1], at_x(lax.rem(x + d, NX))) for d in range(1, NX)]
    own_v = weight_rows(2, y)
    own_k = weight_rows(1, y)

    z_v = z_send(2, ring_v.total(own_v))
    z_k = z_send(1, ring_k.total(own_k))

    for copy in c_dot:
        copy.wait_recv()
    dot_rows = dots[...] + dotr[0] + dotr[1] + dotr[2]
    dot_all = jnp.broadcast_to(dot_rows[0:1], (HD, TOK)).T
    local["gp"].wait()
    grad_normed = ring_x.total(term_own)
    norm_own = xs[c, 0].astype(F32) * inv_rms
    mean = dot_all[:, 0:1] * (1.0 / D)
    gsb[...] = (gp[...].astype(F32) + inv_rms * (grad_normed - norm_own * mean)).astype(BF)
    out_gs = pltpu.make_async_copy(gsb, gs_o.at[0], osem.at[1])
    out_gs.start()
    c_fi.wait_recv()
    out_fi2 = pltpu.make_async_copy(fic, fi_o.at[0, :, others], osem.at[2])
    out_fi2.start()

    z_total(0, z_q)
    z_total(2, z_v)
    z_total(1, z_k)
    out_wg = pltpu.make_async_copy(wgb, wg_o, osem.at[3])
    out_wg.start()
    for copy in (out_fi, out_gs, out_fi2, out_wg):
        copy.wait()
    for copy in pending:
        copy.wait_send()


def hand_out(fi, gs, wg, fi_o, gs_o, q_o, k_o, v_o, fi_v, gs_v, wg_v, isem, osem):
    arrive = [(fi, fi_v), (gs, gs_v), (wg, wg_v)]
    leave = [(fi_v, fi_o), (gs_v, gs_o), (wg_v.at[0], q_o), (wg_v.at[1], k_o), (wg_v.at[2], v_o)]
    taken = [pltpu.make_async_copy(a, b, isem.at[i]) for i, (a, b) in enumerate(arrive)]
    given = [pltpu.make_async_copy(a, b, osem.at[i]) for i, (a, b) in enumerate(leave)]
    for copy in taken:
        copy.start()
    for i in range(2):
        taken[i].wait()
        given[i].start()
    taken[2].wait()
    for copy in given[2:]:
        copy.start()
    for copy in given:
        copy.wait()


def solution(mesh):
    nz = mesh.shape["seq"] // 2
    ny = mesh.shape["dp"]
    rw = D // (2 * nz * ny)
    rows_y = nz * rw
    half = rows_y // 2

    scan = [
        pltpu.VMEM((PIECES, MSG, HD), BF),
        pltpu.VMEM((3, PIECES, MSG, HD), BF),
        pltpu.VMEM((PIECES, MSG, HD), BF),
        pltpu.VMEM((FEAT, HD), BF),
    ]

    def shards(pt, mo, gm, gp, wq, wk, wv, rf, ids):
        total_rows = TOK * 2 * nz * ny
        copies = 110
        stream = jax.ShapeDtypeStruct((1, TOK, WID), BF)
        grads = jax.ShapeDtypeStruct((rw, WID), F32)
        limit = pltpu.CompilerParams(
            collective_id=0, has_side_effects=True, vmem_limit_bytes=58 * 1024 * 1024
        )
        first_in, grad_second, weights = pl.pallas_call(
            functools.partial(kernel, nz, ny, 1.0 / total_rows**0.5),
            out_shape=(stream, stream, jax.ShapeDtypeStruct((3, rw, WID), F32)),
            in_specs=[pl.BlockSpec(memory_space=pl.ANY)] * 9,
            out_specs=[pl.BlockSpec(memory_space=pl.ANY)] * 3,
            scratch_shapes=[
                pltpu.VMEM((2, NX, TOK, WID), BF),
                pltpu.VMEM((2, TOK, HD), BF),
                pltpu.VMEM((2, TOK, HD), BF),
                pltpu.VMEM((TOK, WID), BF),
                pltpu.VMEM((3, D, WID), BF),
                pltpu.VMEM((D, WID), BF),
                pltpu.VMEM((D, HD), BF),
                pltpu.VMEM((HD, FEAT), BF),
                pltpu.VMEM((2, 1, TOK), jnp.int32),
                pltpu.VMEM((2, NX, TOK, WID), BF),
                pltpu.VMEM((ny, rows_y, 2 * TOK), BF),
                pltpu.VMEM((2, TOK, HD), BF),
                pltpu.VMEM((2, TOK, HD), BF),
                pltpu.VMEM((2, TOK, HD), BF),
                pltpu.VMEM((2, TOK, FEAT), BF),
                pltpu.VMEM((2, TOK, FEAT), BF),
                pltpu.VMEM((3, TOK, TOK), BF),
                pltpu.VMEM((3, TOK, TOK), BF),
                pltpu.VMEM((2, TOK, HD), BF),
                pltpu.VMEM((2, TOK, FEAT), F32),
                pltpu.VMEM((2, TOK, HD), F32),
                pltpu.VMEM((3, 2 * TOK, WID), BF),
                pltpu.VMEM((2, TOK, HD), BF),
                pltpu.VMEM((TOK, HD), BF),
                pltpu.VMEM((TOK, WID), BF),
                pltpu.VMEM((3, rw, WID), F32),
                *scan,
                *scan,
                pltpu.VMEM((2, TOK // 2, WID), BF),
                pltpu.VMEM((2, 2, TOK // 2, WID), BF),
                pltpu.VMEM((2, TOK // 2, WID), BF),
                pltpu.VMEM((2, 2, TOK // 2, WID), BF),
                pltpu.VMEM((8, TOK), F32),
                pltpu.VMEM((NX - 1, 8, TOK), F32),
                pltpu.VMEM((3, 2, half, WID), BF),
                pltpu.VMEM((3, 2, 2, half, WID), BF),
                pltpu.VMEM((3, 2, half, WID), BF),
                pltpu.VMEM((3, 2, 2, half, WID), BF),
                pltpu.VMEM((3, nz, 2 * rw, HD), BF),
                pltpu.VMEM((3, nz, 2 * rw, HD), BF),
                pltpu.SemaphoreType.DMA((12,)),
                pltpu.SemaphoreType.DMA((4,)),
                pltpu.SemaphoreType.DMA((copies,)),
                pltpu.SemaphoreType.DMA((copies,)),
            ],
            compiler_params=limit,
            cost_estimate=pl.CostEstimate(
                flops=1_800_000_000, bytes_accessed=4_000_000, transcendentals=300_000
            ),
        )(pt, mo, gm, gp, wq, wk, wv, rf, ids)
        return pl.pallas_call(
            hand_out,
            out_shape=(stream, stream, grads, grads, grads),
            in_specs=[pl.BlockSpec(memory_space=pl.ANY)] * 3,
            out_specs=[pl.BlockSpec(memory_space=pl.ANY)] * 5,
            scratch_shapes=[
                pltpu.VMEM((1, TOK, WID), BF),
                pltpu.VMEM((1, TOK, WID), BF),
                pltpu.VMEM((3, rw, WID), F32),
                pltpu.SemaphoreType.DMA((3,)),
                pltpu.SemaphoreType.DMA((5,)),
            ],
            compiler_params=pltpu.CompilerParams(vmem_limit_bytes=58 * 1024 * 1024),
        )(first_in, grad_second, weights)

    stream = P("dp", "seq", "head")
    return jax.shard_map(
        shards,
        mesh=mesh,
        in_specs=(
            stream,
            stream,
            stream,
            stream,
            P(None, "head"),
            P(None, "head"),
            P(None, "head"),
            P("head", None, None),
            P("dp", "seq"),
        ),
        out_specs=(
            stream,
            stream,
            P(("seq", "dp"), "head"),
            P(("seq", "dp"), "head"),
            P(("seq", "dp"), "head"),
        ),
        check_vma=False,
    )
```

```python
import functools

import jax
import jax.numpy as jnp
from jax import lax
from jax.experimental import pallas as pl
from jax.experimental.pallas import tpu as pltpu
from jax.sharding import PartitionSpec as P

MESH = pl.DeviceIdType.MESH
BF = jnp.bfloat16
F32 = jnp.float32
EPSILON = 1e-06
TOK = 256
D = 1024
WID = 256
HD = 128
FEAT = 256
IDR = 16
PIECES = 2
CUT = FEAT // PIECES
MSG = CUT + IDR
NX = 4


def nn(a, b):
    return jnp.dot(a, b, preferred_element_type=F32)


def nt(a, b):
    return lax.dot_general(a, b, (((1,), (1,)), ((), ())), preferred_element_type=F32)


def tn(a, b):
    return lax.dot_general(a, b, (((0,), (0,)), ((), ())), preferred_element_type=F32)


def kernel(
    nz,
    ny,
    grad_scale,
    pt_h,
    mo_h,
    gm_h,
    gp_h,
    wq_h,
    wk_h,
    wv_h,
    rf_h,
    ids_h,
    fi_o,
    gs_o,
    wg_o,
    xs,
    moh,
    gmh,
    gp,
    w3,
    wkv,
    wqc,
    rf,
    ids,
    nrm,
    ntp,
    qb,
    kb,
    vb,
    fq,
    fk,
    pair,
    dpr,
    ga,
    dfk,
    dvl,
    dh,
    fib,
    fic,
    gsb,
    wgb,
    fmsg,
    fgot,
    ftwo,
    fst,
    bmsg,
    bgot,
    btwo,
    bst,
    xso,
    xsm,
    xro,
    xrm,
    dots,
    dotr,
    yso,
    ysm,
    yro,
    yrm,
    zs,
    zr,
    lsem,
    osem,
    ssem,
    rsem,
    know,
):
    seq = lax.axis_index("seq")
    x = lax.axis_index("head")
    y = lax.axis_index("dp")
    z = seq // 2
    c = seq % 2
    oc = 1 - c
    rw = D // (2 * nz * ny)
    right = lax.rem(x + 1, NX)
    left = lax.rem(x + NX - 1, NX)
    opp = lax.rem(x + 2, NX)
    up, down = lax.rem(y + 1, ny), lax.rem(y + ny - 1, ny)

    def at_x(other):
        return (seq, other, y)

    def at_y(other):
        return (seq, x, other)

    def at_z(step):
        return (lax.rem(z + step + nz, nz) * 2 + c, x, y)

    sibling = (z * 2 + oc, x, y)

    barrier = pltpu.get_barrier_semaphore()
    peers = [at_x(lax.rem(x + d, NX)) for d in range(1, NX)]
    peers += [sibling]
    peers += [at_z(d) for d in (1, nz - 1, 2, nz - 2)]
    peers += [at_y(lax.rem(y + d, ny)) for d in range(1, ny)]
    for peer in peers:
        pl.semaphore_signal(barrier, inc=1, device_id=peer, device_id_type=MESH)

    mine = pl.ds(pl.multiple_of(c * HD, HD), HD)
    others = pl.ds(pl.multiple_of(oc * HD, HD), HD)
    local = {}
    for i, (name, src, dst) in enumerate(
        [
            ("pt", pt_h.at[0], xs.at[c, 0]),
            ("ids", ids_h, ids.at[c]),
            ("wk", wk_h.at[:, mine], wkv.at[:, pl.ds(0, HD)]),
            ("wv", wv_h.at[:, mine], wkv.at[:, pl.ds(HD, HD)]),
            ("rf", rf_h.at[c], rf),
            ("wq", wq_h.at[:, mine], wqc),
            ("gm", gm_h.at[0, :, mine], gmh.at[c]),
            ("mo", mo_h.at[0, :, mine], moh.at[c]),
            ("w0", wq_h, w3.at[0]),
            ("w1", wk_h, w3.at[1]),
            ("w2", wv_h, w3.at[2]),
            ("gp", gp_h.at[0], gp),
        ]
    ):
        local[name] = pltpu.make_async_copy(src, dst, lsem.at[i])

    counter = [0]
    pending = []

    def send(src, dst, device):
        i = counter[0]
        counter[0] += 1
        copy = pltpu.make_async_remote_copy(
            src_ref=src,
            dst_ref=dst,
            send_sem=ssem.at[i],
            recv_sem=rsem.at[i],
            device_id=device,
            device_id_type=MESH,
        )
        copy.start()
        pending.append(copy)
        return copy

    early = ("pt", "ids")
    for name in early:
        local[name].start()
    pl.semaphore_wait(barrier, len(peers))

    top, bot = pl.ds(0, TOK // 2), pl.ds(TOK // 2, TOK // 2)
    l_top = send(pt_h.at[0, top], xs.at[c, 1, top], at_x(right))
    r_bot = send(pt_h.at[0, bot], xs.at[c, 3, bot], at_x(left))
    l_bot = send(pt_h.at[0, bot], xs.at[c, 1, bot], at_x(right))
    r_top = send(pt_h.at[0, top], xs.at[c, 3, top], at_x(left))
    passed = [send(pt_h.at[0], xs.at[c, 0], sibling)]
    c_ids = send(ids_h, ids.at[c], sibling)
    for name, copy in local.items():
        if name not in early:
            copy.start()
    for i, step in enumerate((2, -2)):
        pl.semaphore_signal(know.at[i], inc=1, device_id=at_z(step), device_id_type=MESH)
    c_gm = send(gm_h.at[0, :, others], gmh.at[c], sibling)
    c_mo = send(mo_h.at[0, :, others], moh.at[c], sibling)

    def pass_on(slot, rows):
        passed.append(send(xs.at[c, slot, rows], xs.at[c, slot, rows], sibling))

    l_top.wait_recv()
    o_top = send(xs.at[c, 1, top], xs.at[c, 2, top], at_x(right))
    pass_on(1, top)
    r_bot.wait_recv()
    o_bot = send(xs.at[c, 3, bot], xs.at[c, 2, bot], at_x(left))
    pass_on(3, bot)

    local["ids"].wait()
    c_ids.wait_recv()
    row_ids, col_ids = [], []
    for b in range(2):
        row_ids.append(jnp.broadcast_to(ids[b].astype(F32), (TOK, TOK)))
        col_ids.append(row_ids[b].T)
    tri = lax.broadcasted_iota(jnp.int32, (TOK, TOK), 0) >= lax.broadcasted_iota(
        jnp.int32, (TOK, TOK), 1
    )
    chip_last = row_ids[1][:, TOK - 1 : TOK]
    chip_first = row_ids[0][:, 0:1]
    last_rows = jnp.broadcast_to(chip_last[:IDR], (IDR, HD)).astype(BF)
    first_rows = jnp.broadcast_to(chip_first[:IDR], (IDR, HD)).astype(BF)
    for i in range(PIECES):
        fmsg[i, CUT:MSG] = last_rows
        bmsg[i, CUT:MSG] = first_rows

    def on_rows(b, ident):
        return col_ids[b][:, :HD] == ident

    def square_sum(b, slot):
        wide = xs[b, slot].astype(F32)
        return jnp.sum(wide * wide, axis=1, keepdims=True)

    def normalize(b, squares):
        inv = lax.rsqrt(squares * (1.0 / D) + EPSILON)
        for slot in range(NX):
            nrm[b, slot] = (xs[b, slot].astype(F32) * inv).astype(BF)
        return inv

    def source(slot):
        return lax.rem(x + NX - slot, NX)

    def project(b, weights):
        total = None
        for slot in range(NX):
            rows = pl.ds(pl.multiple_of(source(slot) * WID, WID), WID)
            term = nn(nrm[b, slot], weights[rows, :])
            total = term if total is None else total + term
        return total.astype(BF)

    def features(projected):
        wide = projected.astype(F32)
        norm = jnp.sum(wide * wide, axis=1, keepdims=True)
        exponent = nn(projected, rf[...]) * (1.0 / HD**0.25) - norm * (1.0 / (2.0 * HD**0.5))
        return (jnp.exp(exponent) * (1.0 / FEAT**0.5)).astype(BF)

    def keys_values(b):
        both = project(b, wkv)
        kb[b] = both[:, :HD]
        vb[b] = both[:, HD:]
        fk[b] = features(both[:, :HD])

    local["pt"].wait()
    squares = square_sum(c, 0)
    l_bot.wait_recv()
    pass_on(1, bot)
    r_top.wait_recv()
    pass_on(3, top)
    squares = squares + square_sum(c, 1) + square_sum(c, 3)
    o_top.wait_recv()
    pass_on(2, top)
    o_bot.wait_recv()
    pass_on(2, bot)
    squares = squares + square_sum(c, 2)
    inv_rms = normalize(c, squares)
    local["wk"].wait()
    local["wv"].wait()
    local["rf"].wait()
    keys_values(c)
    for copy in passed:
        copy.wait_recv()
    squares = square_sum(oc, 0) + square_sum(oc, 1) + square_sum(oc, 3) + square_sum(oc, 2)
    normalize(oc, squares)
    keys_values(oc)

    def outer_sum(left_ref, right_ref, ident):
        total = None
        for b in range(2):
            masked = jnp.where(on_rows(b, ident), right_ref[b].astype(F32), 0.0).astype(BF)
            term = tn(left_ref[b], masked)
            total = term if total is None else total + term
        return total.astype(BF)

    def merge(near, far):
        return near[:CUT] + jnp.where(near[CUT : CUT + 1] == far[CUT : CUT + 1], far[:CUT], 0.0)

    class Scan:
        def __init__(self, sign, msg, got, two, state):
            self.sign, self.msg, self.got, self.two, self.state = sign, msg, got, two, state

        def begin(self, outer):
            self.near, self.far = [], []
            for i in range(PIECES):
                self.msg[i, 0:CUT] = outer[i * CUT : (i + 1) * CUT]
                self.near.append(send(self.msg.at[i], self.got.at[0, i], at_z(self.sign)))
                self.far.append(send(self.msg.at[i], self.got.at[1, i], at_z(2 * self.sign)))

        def pairs(self):
            self.last = []
            for i in range(PIECES):
                self.near[i].wait_recv()
                self.far[i].wait_recv()
                near, far = self.got[0, i].astype(F32), self.got[1, i].astype(F32)
                self.two[i, 0:CUT] = merge(near, far).astype(BF)
                self.two[i, CUT:MSG] = self.got[0, i, CUT:MSG]
                self.last.append(send(self.two.at[i], self.got.at[2, i], at_z(2 * self.sign)))

        def finish(self):
            for i in range(PIECES):
                self.last[i].wait_recv()
                near, far = self.two[i].astype(F32), self.got[2, i].astype(F32)
                self.state[i * CUT : (i + 1) * CUT] = merge(near, far).astype(BF)
            return self.two[0, CUT : CUT + 1].astype(F32)

    forward = Scan(1, fmsg, fgot, ftwo, fst)
    forward.begin(outer_sum(fk, vb, chip_last))
    for i in range(2):
        pl.semaphore_wait(know.at[i], 1)
    if nz > 4:
        for i, step in enumerate((4, -4)):
            pl.semaphore_signal(know.at[2 + i], inc=1, device_id=at_z(step), device_id_type=MESH)

    local["wq"].wait()
    for b in range(2):
        qb[b] = project(b, wqc)
        fq[b] = features(qb[b])

    forward.pairs()

    blocks = [(0, 0), (1, 0), (1, 1)]
    allowed = []
    for i, (b, s) in enumerate(blocks):
        same = row_ids[s] == col_ids[b]
        allowed.append(same & tri if b == s else same)
        pair[i] = jnp.where(allowed[i], nt(fq[b], fk[s]), 0.0).astype(BF)
    attn = [nn(pair[0], vb[0]), nn(pair[1], vb[0]) + nn(pair[2], vb[1])]

    per_slot = nz // NX
    for slot in range(NX):
        place = pl.ds(pl.multiple_of(source(slot) * (per_slot * rw), per_slot * rw), per_slot * rw)
        for b in range(2):
            turned = nrm[b, slot].astype(F32).T.reshape(per_slot, 2, ny, rw, TOK)
            turned = jnp.where(c == 0, turned[:, 0], turned[:, 1])
            for part in range(ny):
                block = turned[:, part].reshape(per_slot * rw, TOK)
                ntp[part, place, b * TOK : (b + 1) * TOK] = block.astype(BF)

    local["gm"].wait()
    local["mo"].wait()
    c_gm.wait_recv()
    c_mo.wait_recv()
    f_id = forward.finish()

    acts = []
    for b in range(2):
        attention = attn[b] + jnp.where(on_rows(b, f_id), nn(fq[b], fst[...]), 0.0)
        inv_attn = lax.rsqrt(jnp.mean(attention * attention, axis=1, keepdims=True) + EPSILON)
        act = attention * inv_attn
        acts.append(act)
        grad_act = gmh[b].astype(F32)
        inner = jnp.mean(grad_act * act, axis=1, keepdims=True)
        ga[b] = (inv_attn * (grad_act - act * inner)).astype(BF)

    backward = Scan(-1, bmsg, bgot, btwo, bst)
    backward.begin(outer_sum(fq, ga, chip_first))

    def feature_grad(dfeature, feature, projected):
        dexponent = dfeature * feature.astype(F32)
        back = nt(dexponent.astype(BF), rf[...])
        totals = jnp.sum(dexponent, axis=1, keepdims=True)
        result = back * (1.0 / HD**0.25) - projected.astype(F32) * (totals * (1.0 / HD**0.5))
        return result.astype(BF)

    for i, (b, s) in enumerate(blocks):
        dpr[i] = jnp.where(allowed[i], nt(ga[b], vb[s]), 0.0).astype(BF)
    dfq = [nn(dpr[0], fk[0]), nn(dpr[1], fk[0]) + nn(dpr[2], fk[1])]

    for b in range(2):
        masked = jnp.where(on_rows(b, f_id), ga[b].astype(F32), 0.0).astype(BF)
        dfeat = dfq[b] + nt(masked, fst[...])
        dh[0, b * TOK : (b + 1) * TOK, mine] = feature_grad(dfeat, fq[b], qb[b])
    c_dq = send(dh.at[0, :, mine], dh.at[0, :, mine], sibling)

    dfk[0] = tn(dpr[0], fq[0]) + tn(dpr[1], fq[1])
    dfk[1] = tn(dpr[2], fq[1])
    dvl[0] = tn(pair[0], ga[0]) + tn(pair[1], ga[1])
    dvl[1] = tn(pair[2], ga[1])

    backward.pairs()

    class Ring:
        def __init__(self, so, sm, ro, rm, to_right, to_left):
            self.so, self.sm, self.ro, self.rm = so, sm, ro, rm
            self.to_right, self.to_left = to_right, to_left
            self.half = so.shape[1]

        def opposite(self, block):
            self.so[0] = block[: self.half].astype(BF)
            self.o0 = send(self.so.at[0], self.ro.at[0], self.to_right)
            self.so[1] = block[self.half :].astype(BF)
            self.o1 = send(self.so.at[1], self.ro.at[1], self.to_left)

        def sides(self, to_right, to_left):
            self.sm[0, 1] = to_right[self.half :].astype(BF)
            self.m01 = send(self.sm.at[0, 1], self.rm.at[0, 1], self.to_right)
            self.sm[1, 0] = to_left[: self.half].astype(BF)
            self.m10 = send(self.sm.at[1, 0], self.rm.at[1, 0], self.to_left)
            self.r_top = to_right[: self.half]
            self.l_bot = to_left[self.half :]

        def relay(self):
            self.o0.wait_recv()
            self.sm[0, 0] = (self.r_top + self.ro[0].astype(F32)).astype(BF)
            self.m00 = send(self.sm.at[0, 0], self.rm.at[0, 0], self.to_right)
            self.o1.wait_recv()
            self.sm[1, 1] = (self.l_bot + self.ro[1].astype(F32)).astype(BF)
            self.m11 = send(self.sm.at[1, 1], self.rm.at[1, 1], self.to_left)

        def total(self, own):
            for copy in (self.m01, self.m10, self.m00, self.m11):
                copy.wait_recv()
            halves = [
                own[i * self.half : (i + 1) * self.half]
                + self.rm[0, i].astype(F32)
                + self.rm[1, i].astype(F32)
                for i in range(2)
            ]
            return jnp.concatenate(halves, axis=0)

    def y_ring(which):
        return Ring(yso.at[which], ysm.at[which], yro.at[which], yrm.at[which], at_y(up), at_y(down))

    def weight_rows(which, part):
        return nn(ntp[part], dh[which]) * grad_scale

    def start_weights(which):
        ring = y_ring(which)
        ring.opposite(weight_rows(which, lax.rem(y + 2, ny)))
        ring.sides(weight_rows(which, up), weight_rows(which, down))
        return ring

    def z_send(which, total):
        split = total.reshape(nz, rw, WID)
        zs[which] = jnp.concatenate([split[:, :, :HD], split[:, :, HD:]], axis=1).astype(BF)
        copies = []
        for d in range(1, nz):
            to = lax.rem(z + d, nz)
            copies.append(send(zs.at[which, to], zr.at[which, d], at_z(d)))
        return copies

    def z_total(which, copies):
        total = zs[which, z].astype(F32)
        for d in range(1, nz):
            copies[d - 1].wait_recv()
            total = total + zr[which, d].astype(F32)
        wgb[which] = jnp.concatenate([total[:rw], total[rw:]], axis=1)

    c_dq.wait_recv()
    ring_q = start_weights(0)

    for b in range(2):
        fib[b] = (moh[b].astype(F32) - acts[b]).astype(BF)
    c_fi = send(fib.at[oc], fic, sibling)
    out_fi = pltpu.make_async_copy(fib.at[c], fi_o.at[0, :, mine], osem.at[0])
    out_fi.start()

    own_q = weight_rows(0, y)
    ring_q.relay()

    b_id = backward.finish()

    for b in range(2):
        carried = jnp.where(on_rows(b, b_id), nn(fk[b], bst[...]), 0.0)
        dh[2, b * TOK : (b + 1) * TOK, mine] = (dvl[b] + carried).astype(BF)
    c_dv = send(dh.at[2, :, mine], dh.at[2, :, mine], sibling)
    for b in range(2):
        masked = jnp.where(on_rows(b, b_id), vb[b].astype(F32), 0.0).astype(BF)
        dfeat = dfk[b] + nt(masked, bst[...])
        dh[1, b * TOK : (b + 1) * TOK, mine] = feature_grad(dfeat, fk[b], kb[b])
    c_dk = send(dh.at[1, :, mine], dh.at[1, :, mine], sibling)
    if nz > 4:
        for i in range(2):
            pl.semaphore_wait(know.at[2 + i], 1)
    z_q = z_send(0, ring_q.total(own_q))
    local["w0"].wait()
    local["w1"].wait()
    local["w2"].wait()

    c_dv.wait_recv()
    ring_v = start_weights(2)
    c_dk.wait_recv()
    ring_k = start_weights(1)

    own_rows = pl.ds(pl.multiple_of(c * TOK, TOK), TOK)

    def normed_term(owner, slot):
        rows = pl.ds(pl.multiple_of(owner * WID, WID), WID)
        term = nt(dh[0, own_rows, :], w3[0, rows, :])
        term = term + nt(dh[1, own_rows, :], w3[1, rows, :])
        term = term + nt(dh[2, own_rows, :], w3[2, rows, :])
        return term, jnp.sum(term * xs[c, slot].astype(F32), axis=1, keepdims=True)

    ring_x = Ring(xso, xsm, xro, xrm, at_x(right), at_x(left))
    term, dot = normed_term(opp, 2)
    ring_x.opposite(term)
    term_r, dot_r = normed_term(right, 3)
    term_l, dot_l = normed_term(left, 1)
    ring_x.sides(term_r, term_l)

    ring_v.relay()
    ring_k.relay()
    ring_x.relay()

    term_own, dot_own = normed_term(x, 0)
    dot = (dot + dot_r + dot_l + dot_own) * inv_rms
    dots[...] = jnp.broadcast_to(dot, (TOK, HD)).T[:8]
    c_dot = [send(dots, dotr.at[d - 1], at_x(lax.rem(x + d, NX))) for d in range(1, NX)]
    own_v = weight_rows(2, y)
    own_k = weight_rows(1, y)

    z_v = z_send(2, ring_v.total(own_v))
    z_k = z_send(1, ring_k.total(own_k))

    for copy in c_dot:
        copy.wait_recv()
    dot_rows = dots[...] + dotr[0] + dotr[1] + dotr[2]
    dot_all = jnp.broadcast_to(dot_rows[0:1], (HD, TOK)).T
    local["gp"].wait()
    grad_normed = ring_x.total(term_own)
    norm_own = xs[c, 0].astype(F32) * inv_rms
    mean = dot_all[:, 0:1] * (1.0 / D)
    gsb[...] = (gp[...].astype(F32) + inv_rms * (grad_normed - norm_own * mean)).astype(BF)
    out_gs = pltpu.make_async_copy(gsb, gs_o.at[0], osem.at[1])
    out_gs.start()
    c_fi.wait_recv()
    out_fi2 = pltpu.make_async_copy(fic, fi_o.at[0, :, others], osem.at[2])
    out_fi2.start()

    z_total(0, z_q)
    z_total(2, z_v)
    z_total(1, z_k)
    out_wg = pltpu.make_async_copy(wgb, wg_o, osem.at[3])
    out_wg.start()
    for copy in (out_fi, out_gs, out_fi2, out_wg):
        copy.wait()
    for copy in pending:
        copy.wait_send()


def hand_out(fi, gs, wg, fi_o, gs_o, q_o, k_o, v_o, fi_v, gs_v, wg_v, isem, osem):
    arrive = [(fi, fi_v), (gs, gs_v), (wg, wg_v)]
    leave = [(fi_v, fi_o), (gs_v, gs_o), (wg_v.at[0], q_o), (wg_v.at[1], k_o), (wg_v.at[2], v_o)]
    taken = [pltpu.make_async_copy(a, b, isem.at[i]) for i, (a, b) in enumerate(arrive)]
    given = [pltpu.make_async_copy(a, b, osem.at[i]) for i, (a, b) in enumerate(leave)]
    for copy in taken:
        copy.start()
    for i in range(2):
        taken[i].wait()
        given[i].start()
    taken[2].wait()
    for copy in given[2:]:
        copy.start()
    for copy in given:
        copy.wait()


def solution(mesh):
    nz = mesh.shape["seq"] // 2
    ny = mesh.shape["dp"]
    rw = D // (2 * nz * ny)
    rows_y = nz * rw
    half = rows_y // 2

    scan = [
        pltpu.VMEM((PIECES, MSG, HD), BF),
        pltpu.VMEM((3, PIECES, MSG, HD), BF),
        pltpu.VMEM((PIECES, MSG, HD), BF),
        pltpu.VMEM((FEAT, HD), BF),
    ]

    def shards(pt, mo, gm, gp, wq, wk, wv, rf, ids):
        total_rows = TOK * 2 * nz * ny
        copies = 110
        stream = jax.ShapeDtypeStruct((1, TOK, WID), BF)
        grads = jax.ShapeDtypeStruct((rw, WID), F32)
        limit = pltpu.CompilerParams(
            collective_id=0, has_side_effects=True, vmem_limit_bytes=58 * 1024 * 1024
        )
        first_in, grad_second, weights = pl.pallas_call(
            functools.partial(kernel, nz, ny, 1.0 / total_rows**0.5),
            out_shape=(stream, stream, jax.ShapeDtypeStruct((3, rw, WID), F32)),
            in_specs=[pl.BlockSpec(memory_space=pl.ANY)] * 9,
            out_specs=[pl.BlockSpec(memory_space=pl.ANY)] * 3,
            scratch_shapes=[
                pltpu.VMEM((2, NX, TOK, WID), BF),
                pltpu.VMEM((2, TOK, HD), BF),
                pltpu.VMEM((2, TOK, HD), BF),
                pltpu.VMEM((TOK, WID), BF),
                pltpu.VMEM((3, D, WID), BF),
                pltpu.VMEM((D, WID), BF),
                pltpu.VMEM((D, HD), BF),
                pltpu.VMEM((HD, FEAT), BF),
                pltpu.VMEM((2, 1, TOK), jnp.int32),
                pltpu.VMEM((2, NX, TOK, WID), BF),
                pltpu.VMEM((ny, rows_y, 2 * TOK), BF),
                pltpu.VMEM((2, TOK, HD), BF),
                pltpu.VMEM((2, TOK, HD), BF),
                pltpu.VMEM((2, TOK, HD), BF),
                pltpu.VMEM((2, TOK, FEAT), BF),
                pltpu.VMEM((2, TOK, FEAT), BF),
                pltpu.VMEM((3, TOK, TOK), BF),
                pltpu.VMEM((3, TOK, TOK), BF),
                pltpu.VMEM((2, TOK, HD), BF),
                pltpu.VMEM((2, TOK, FEAT), F32),
                pltpu.VMEM((2, TOK, HD), F32),
                pltpu.VMEM((3, 2 * TOK, WID), BF),
                pltpu.VMEM((2, TOK, HD), BF),
                pltpu.VMEM((TOK, HD), BF),
                pltpu.VMEM((TOK, WID), BF),
                pltpu.VMEM((3, rw, WID), F32),
                *scan,
                *scan,
                pltpu.VMEM((2, TOK // 2, WID), BF),
                pltpu.VMEM((2, 2, TOK // 2, WID), BF),
                pltpu.VMEM((2, TOK // 2, WID), BF),
                pltpu.VMEM((2, 2, TOK // 2, WID), BF),
                pltpu.VMEM((8, TOK), F32),
                pltpu.VMEM((NX - 1, 8, TOK), F32),
                pltpu.VMEM((3, 2, half, WID), BF),
                pltpu.VMEM((3, 2, 2, half, WID), BF),
                pltpu.VMEM((3, 2, half, WID), BF),
                pltpu.VMEM((3, 2, 2, half, WID), BF),
                pltpu.VMEM((3, nz, 2 * rw, HD), BF),
                pltpu.VMEM((3, nz, 2 * rw, HD), BF),
                pltpu.SemaphoreType.DMA((12,)),
                pltpu.SemaphoreType.DMA((4,)),
                pltpu.SemaphoreType.DMA((copies,)),
                pltpu.SemaphoreType.DMA((copies,)),
                pltpu.SemaphoreType.REGULAR((4,)),
            ],
            compiler_params=limit,
            cost_estimate=pl.CostEstimate(
                flops=1_800_000_000, bytes_accessed=4_000_000, transcendentals=300_000
            ),
        )(pt, mo, gm, gp, wq, wk, wv, rf, ids)
        return pl.pallas_call(
            hand_out,
            out_shape=(stream, stream, grads, grads, grads),
            in_specs=[pl.BlockSpec(memory_space=pl.ANY)] * 3,
            out_specs=[pl.BlockSpec(memory_space=pl.ANY)] * 5,
            scratch_shapes=[
                pltpu.VMEM((1, TOK, WID), BF),
                pltpu.VMEM((1, TOK, WID), BF),
                pltpu.VMEM((3, rw, WID), F32),
                pltpu.SemaphoreType.DMA((3,)),
                pltpu.SemaphoreType.DMA((5,)),
            ],
            compiler_params=pltpu.CompilerParams(vmem_limit_bytes=58 * 1024 * 1024),
        )(first_in, grad_second, weights)

    stream = P("dp", "seq", "head")
    return jax.shard_map(
        shards,
        mesh=mesh,
        in_specs=(
            stream,
            stream,
            stream,
            stream,
            P(None, "head"),
            P(None, "head"),
            P(None, "head"),
            P("head", None, None),
            P("dp", "seq"),
        ),
        out_specs=(
            stream,
            stream,
            P(("seq", "dp"), "head"),
            P(("seq", "dp"), "head"),
            P(("seq", "dp"), "head"),
        ),
        check_vma=False,
    )
```
